256 devices in a mesh: fsdp: 64 (over z, x, y_hi), seq: 4 (over y_lo, core).
Axes of the slice: x: 4, y: 4 (y_hi: 2, y_lo: 2; y = y_hi * 2 + y_lo), z: 8, core: 2. Of those that a mesh axis runs over, the one named last changes fastest.
Arguments:
- layer_input: bfloat16 [32768, 4096], P(('fsdp', 'seq')), may hold values from -6 to 6
- head_input: bfloat16 [32768, 4096], P(('fsdp', 'seq')), may hold values from -6 to 6
- targets: bfloat16 [32768, 4096], P(('fsdp', 'seq')), may hold values from -6 to 6
- proj_weight: bfloat16 [4096, 640], P('fsdp'), may hold values from -0.09375 to 0.09375
- rates: float32 [2, 64], replicated, may hold values from 0.001 to 0.05
- dt_bias: float32 [2, 64], replicated, may hold values from -1 to 1
- mask_index: int32 [64, 204], P('fsdp'), may hold values from 0 to 511, as said below
Outputs:
- grad_x: bfloat16 [32768, 4096], P(('fsdp', 'seq'))
- grad_input: bfloat16 [32768, 4096], P(('fsdp', 'seq'))
- grad_weight: float32 [4096, 640], P('fsdp')
The draws below stay inside these ranges and needn't reach their ends.
Inputs may be any that keep to these rules, and one draw needn't show every extreme that they name: `mask_index`: row i holds 204 distinct positions within image i.
All inputs are finite; a program needn't handle non-finite values.
Results may differ from the reference program's by a relative error of at most 0.015.
Values may be sent and summed in bfloat16 or wider, within the bound.
No kernel may reach another device: no remote copies, remote signals or barrier semaphores. Data moves between devices by JAX's collectives and lax.ppermute only.
A program may use at most 128 MiB of HBM per device.

```python
import math
import jax
import jax.numpy as jnp
from jax import lax

D = 4096
H = 64
N = 128
P_SIZE = 64
TOK_DEV = 128
LENGTH = 512
IMAGES = 64
MASKED = 204
TOKENS = 32768
N_SEQ = 4


def draw_mask_index(key, part):
    key = jax.random.fold_in(key, 7)
    row_keys = jax.random.split(key, IMAGES)

    def one_row(row_key):
        return jax.random.permutation(row_key, LENGTH)[:MASKED]
    return jax.vmap(one_row)(row_keys).astype(jnp.int32)


def level_of(stream_key, shape, cuts, smallest, high):
    def one(axis_at, shards_of):
        heights = jax.random.uniform(jax.random.fold_in(jax.random.fold_in(stream_key, 6), axis_at), (shards_of,), jnp.float32, smallest / len(cuts), high / len(cuts))
        return jnp.repeat(jnp.exp(heights), shape[axis_at] // shards_of).reshape((-1,) + (1,) * (len(shape) - axis_at - 1))

    level = one(*cuts[0])
    for cut in cuts[1:]:
        level = level * one(*cut)
    return level


def gaussian(own_key, shape, scale, reach, cuts=(), dtype=jnp.bfloat16):
    loudness = level_of(own_key, shape, cuts, -0.22, 0.18) if cuts else 1.0
    entries = jax.random.normal(own_key, shape, jnp.float32) * scale * loudness
    return jnp.minimum(jnp.maximum(entries, -reach), reach).astype(dtype)


def setup_inputs(seed: int = 0) -> dict:
    key_list = jax.random.split(jax.random.key(seed), 8)
    layer_input = gaussian(key_list[0], (TOKENS, D), 1.0, 6.0, ((0, 256),))
    head_input = gaussian(key_list[1], (TOKENS, H * P_SIZE), 1.0, 6.0, ((0, 256),))
    targets = gaussian(key_list[2], (TOKENS, H * P_SIZE), 1.0, 6.0, ((0, 256),))
    proj_weight = gaussian(key_list[3], (D, 4 * N + 2 * H), D ** -0.5, 0.09375, ((0, 64),))
    rates = jnp.clip(jnp.exp(jax.random.uniform(key_list[4], (2, H), jnp.float32, math.log(0.001), math.log(0.05))), 0.001, 0.05)
    dt_bias = jnp.clip(jax.random.uniform(key_list[5], (2, H), jnp.float32, -1.0, 1.0), -1.0, 1.0)
    mask_index = draw_mask_index(jax.random.fold_in(key_list[7], 71), 0)
    return dict(layer_input=layer_input, head_input=head_input, targets=targets, proj_weight=proj_weight, rates=rates, dt_bias=dt_bias, mask_index=mask_index)


HIGHEST_PRECISION = lax.Precision.HIGHEST
EPSILON = 1e-06

def contract(form, left, right):
    return jnp.einsum(form, left.astype(jnp.float32), right.astype(jnp.float32))

def triangle(count, lower):
    row_index = jnp.arange(count)[:, None]
    col_index = jnp.arange(count)[None, :]
    return col_index <= row_index if lower else col_index >= row_index

def prepare(projected, x_heads, rate, bias, course, mask_f, head_count, state_size):
    b_rows = projected[:, 2 * course * state_size:(2 * course + 1) * state_size].astype(jnp.bfloat16)
    c_rows = projected[:, (2 * course + 1) * state_size:(2 * course + 2) * state_size].astype(jnp.bfloat16)
    first_col = 4 * state_size + course * head_count
    z = projected[:, first_col:first_col + head_count] + bias
    step_size = jax.nn.softplus(z)
    g = -rate * step_size
    k = jnp.dot(mask_f, g, precision=HIGHEST_PRECISION)
    block_sum = lax.optimization_barrier(jnp.sum(g, axis=0))
    v = (step_size[:, :, None] * x_heads.astype(jnp.float32)).astype(jnp.bfloat16)
    return (b_rows, c_rows, z, step_size, k, block_sum, v)

def decay_table(k, tri_mask):
    k_heads = k.T
    gaps = k_heads[:, :, None] - k_heads[:, None, :]
    return jnp.where(tri_mask[None], jnp.exp(jnp.where(tri_mask[None], gaps, 0.0)), 0.0)

def block_local(k, block_sum, b_rows, v):
    e_rows = (jnp.exp(block_sum[None, :] - k)[:, :, None] * b_rows[:, None, :].astype(jnp.float32)).astype(jnp.bfloat16)
    return (jnp.exp(block_sum), contract('shp,shn->hpn', v, e_rows))

def block_output(k, tri_mask, b_rows, c_rows, v, entering):
    gram = jnp.dot(c_rows, b_rows.T, preferred_element_type=jnp.float32)
    weights = (decay_table(k, tri_mask) * gram[None]).astype(jnp.bfloat16)
    within = contract('hts,shp->thp', weights, v)
    carried = contract('tn,hpn->thp', c_rows, entering.astype(jnp.bfloat16))
    return within + jnp.exp(k)[:, :, None] * carried

def block_direct(k, grad_out, c_rows):
    scaled = (jnp.exp(k)[:, :, None] * grad_out.astype(jnp.float32)).astype(jnp.bfloat16)
    return (scaled, contract('thp,tn->hpn', scaled, c_rows))

def block_backward(k, block_sum, tri_mask, b_rows, c_rows, v, entering, grad_out, scaled, adjoint):
    gram = jnp.dot(c_rows, b_rows.T, preferred_element_type=jnp.float32)
    decays = decay_table(k, tri_mask)
    weights = (decays * gram[None]).astype(jnp.bfloat16)
    state_half = entering.astype(jnp.bfloat16)
    adjoint_half = adjoint.astype(jnp.bfloat16)
    e_rows = (jnp.exp(block_sum[None, :] - k)[:, :, None] * b_rows[:, None, :].astype(jnp.float32)).astype(jnp.bfloat16)
    grad_v = contract('hts,thp->shp', weights, grad_out) + contract('shn,hpn->shp', e_rows, adjoint_half)
    grad_w = contract('thp,shp->hts', grad_out, v) * decays
    grad_gram = lax.optimization_barrier(jnp.sum(grad_w, axis=0)).astype(jnp.bfloat16)
    weighted = grad_w * gram[None]
    grad_k = (lax.optimization_barrier(jnp.sum(weighted, axis=2)) - lax.optimization_barrier(jnp.sum(weighted, axis=1))).T
    carried = contract('tn,hpn->thp', c_rows, state_half)
    grad_k = grad_k + jnp.exp(k) * lax.optimization_barrier(jnp.sum(grad_out.astype(jnp.float32) * carried, axis=2))
    grad_c = jnp.dot(grad_gram, b_rows, preferred_element_type=jnp.float32) + contract('thp,hpn->tn', scaled, state_half)
    grad_e = contract('shp,hpn->shn', v, adjoint_half)
    factor = jnp.exp(block_sum[None, :] - k)
    grad_b = jnp.dot(grad_gram.T, c_rows, preferred_element_type=jnp.float32) + lax.optimization_barrier(jnp.sum(factor[:, :, None] * grad_e, axis=1))
    r = lax.optimization_barrier(jnp.sum(grad_e * e_rows.astype(jnp.float32), axis=2))
    grad_sum = lax.optimization_barrier(jnp.sum(r, axis=0)) + jnp.exp(block_sum) * lax.optimization_barrier(jnp.sum(adjoint * entering, axis=(1, 2)))
    grad_k = grad_k - r
    grad_g = jnp.dot(tri_mask.astype(jnp.float32).T, grad_k, precision=HIGHEST_PRECISION) + grad_sum[None, :]
    return (grad_v, grad_b, grad_c, grad_g)

def loss_grad(y, goal_rows, masked):
    goal = goal_rows.astype(jnp.float32)
    y_scale = jnp.sqrt(lax.optimization_barrier(jnp.mean(y * y, axis=-1, keepdims=True)) + EPSILON)
    goal_scale = jnp.sqrt(lax.optimization_barrier(jnp.mean(goal * goal, axis=-1, keepdims=True)) + EPSILON)
    cosine = lax.optimization_barrier(jnp.mean(y * goal, axis=-1, keepdims=True)) / (y_scale * goal_scale)
    gradient = (cosine * y / y_scale - goal / goal_scale) / y_scale
    return jnp.where(masked[:, None], gradient, 0.0).astype(jnp.bfloat16)

def carry_chain(decay, members, backward):

    def advance(held, element):
        factor, member = element
        return (factor[:, None, None] * held + member, held)
    anchor = jnp.zeros(members.shape[1:], jnp.float32)
    return lax.scan(advance, anchor, (decay, members), reverse=backward)[1]

def reference(layer_input, head_input, targets, proj_weight, rates, dt_bias, mask_index):
    block_count = N_SEQ
    length = TOK_DEV * N_SEQ
    column_count = 4 * N + 2 * H
    image_input = layer_input.reshape(IMAGES, length, D)
    image_heads = head_input.reshape(IMAGES, block_count, TOK_DEV, H, P_SIZE)
    image_goal = targets.reshape(IMAGES, block_count, TOK_DEV, H * P_SIZE)

    def one_image(running, image_data):
        input_rows, head_blocks, goal_blocks, positions = image_data
        projected = jnp.dot(input_rows, proj_weight, preferred_element_type=jnp.float32).reshape(block_count, TOK_DEV, column_count)
        masked = jnp.any(jnp.arange(length)[:, None] == positions[None, :], axis=1).reshape(block_count, TOK_DEV)
        output_sum = jnp.zeros((block_count, TOK_DEV, H, P_SIZE), jnp.float32)
        kept = []
        for course in range(2):
            tri_mask = triangle(TOK_DEV, course == 0)
            mask_f = tri_mask.astype(jnp.float32)
            rate = rates[course]
            bias = dt_bias[course]
            prepared = jax.vmap(lambda slab, heads_slab: prepare(slab, heads_slab, rate, bias, course, mask_f, H, N))(projected, head_blocks)
            b_rows, c_rows, z, step_size, k, block_sum, v = prepared
            decay, local_state = jax.vmap(block_local)(k, block_sum, b_rows, v)
            entering = carry_chain(decay, local_state, course == 1)
            output_sum = output_sum + jax.vmap(block_output, in_axes=(0, None, 0, 0, 0, 0))(k, tri_mask, b_rows, c_rows, v, entering)
            kept.append((tri_mask, b_rows, c_rows, z, step_size, k, block_sum, v, decay, entering))
        y = output_sum.reshape(block_count, TOK_DEV, H * P_SIZE)
        grad_out = jax.vmap(loss_grad)(y, goal_blocks, masked).reshape(block_count, TOK_DEV, H, P_SIZE)
        grad_x = jnp.zeros((block_count, TOK_DEV, H, P_SIZE), jnp.float32)
        pieces = []
        for course in range(2):
            tri_mask, b_rows, c_rows, z, step_size, k, block_sum, v, decay, entering = kept[course]
            scaled, direct = jax.vmap(block_direct)(k, grad_out, c_rows)
            adjoint = carry_chain(decay, direct, course == 0)
            grad_v, grad_b, grad_c, grad_g = jax.vmap(block_backward, in_axes=(0, 0, None, 0, 0, 0, 0, 0, 0, 0))(k, block_sum, tri_mask, b_rows, c_rows, v, entering, grad_out, scaled, adjoint)
            grad_step = lax.optimization_barrier(jnp.sum(grad_v * head_blocks.astype(jnp.float32), axis=3)) - rates[course] * grad_g
            grad_x = grad_x + step_size[..., None] * grad_v
            pieces.append((grad_b, grad_c, grad_step * jax.nn.sigmoid(z)))
        grad_proj = jnp.concatenate([pieces[0][0], pieces[0][1], pieces[1][0], pieces[1][1], pieces[0][2], pieces[1][2]], axis=-1).astype(jnp.bfloat16).reshape(length, column_count)
        grad_input = jnp.dot(grad_proj, proj_weight.T, preferred_element_type=jnp.float32).astype(jnp.bfloat16)
        running = running + jnp.dot(input_rows.T, grad_proj, preferred_element_type=jnp.float32)
        return (running, (grad_x.astype(jnp.bfloat16).reshape(length, H * P_SIZE), grad_input))
    grad_weight, outputs = lax.scan(one_image, jnp.zeros((D, column_count), jnp.float32), (image_input, image_heads, image_goal, mask_index))
    grad_x, grad_input = outputs
    return (grad_x.reshape(TOKENS, H * P_SIZE), grad_input.reshape(TOKENS, D), grad_weight)
```

```python
import jax
import jax.numpy as jnp
import numpy as np
from jax import lax
from jax.experimental import pallas as pl
from jax.experimental.pallas import tpu as pltpu
from jax.sharding import Mesh
from jax.sharding import PartitionSpec as P

EPSILON = 1e-06
LOG2E = 1.4426950408889634
F32 = jnp.float32
BF16 = jnp.bfloat16
SEQ = ("yl", "c")
VMEM_LIMIT = 56 * 1024 * 1024


def fsdp_axes(count):
    return (count // 8, 4, 2)


def iota(shape, dim):
    return lax.broadcasted_iota(jnp.int32, shape, dim)


def mm(left, right):
    return lax.dot_general(left, right, (((1,), (0,)), ((), ())), preferred_element_type=F32)


def mm_nt(left, right):
    return lax.dot_general(left, right, (((1,), (1,)), ((), ())), preferred_element_type=F32)


def parts(value, count):
    pieces = []
    for _ in range(count):
        piece = value.astype(BF16)
        pieces.append(piece)
        value = value - piece.astype(F32)
    return jnp.concatenate(pieces, axis=1)


def as_bf16(condition):
    return jnp.where(condition, 1.0, 0.0).astype(BF16)


def exact_sum(mask, value):
    width = value.shape[1]
    out = mm(mask, parts(value, 3))
    return out[:, :width] + out[:, width : 2 * width] + out[:, 2 * width :]


def pick(value, chosen, pieces):
    rows, width = value.shape
    table = as_bf16(chosen(iota((pieces * width, width), 0) & (width - 1), iota((pieces * width, width), 1)))
    return mm(parts(value, pieces), table)


def spread_table(pieces, lane_base, lanes):
    shape = (pieces * 128, lanes)
    return as_bf16((iota(shape, 0) & 127) == lane_base + (iota(shape, 1) >> 6))


def prepare_kernel(sel, pa, pb, xh, bias, rate, bc_out, ksp_out, kt_out, fac_out, z_out, state_out):
    tokens = pa.shape[0]
    core, sd = sel[0], sel[1]
    proj = pa[...] + pb[...]
    bc = proj[:, :512].astype(BF16)
    bc_out[...] = bc

    def source(row, col):
        return row == ((col >> 5) & 1) * 64 + core * 32 + (col & 31)

    z = pick(proj[:, 512:640], source, 3) + bias[...]
    z_out[...] = z
    step = jnp.maximum(z, 0.0) + jnp.log1p(jnp.exp(-jnp.abs(z)))
    g = -rate[...] * step * LOG2E
    row = iota((tokens, tokens), 0)
    col = iota((tokens, tokens), 1)
    low = exact_sum(as_bf16(col <= row), g)
    high = exact_sum(as_bf16(col >= row), g)
    lane = iota((tokens, 128), 1)
    first = ((lane >> 5) & 1) == 0
    k = jnp.where(first, low, high)
    total = jnp.where(first[:1], low[tokens - 1 :], high[:1])
    ks = jnp.where(lane < 64, k, step)
    ksp_out[...] = parts(ks, 3)
    kt_out[...] = ks.T
    leaving = jnp.exp2(total - k)
    fac_out[...] = jnp.where(lane < 64, jnp.exp2(k), leaving)
    factor = parts(step * leaving, 2)
    b_t = jnp.where(sd == 0, proj[:, :128], proj[:, 256:384]).T.astype(BF16)
    width = xh.shape[1]
    for at in range(0, width, 256):
        table = spread_table(2, sd * 32 + at // 64, 256)
        ve = (xh[:, at : at + 256].astype(F32) * mm(factor, table)).astype(BF16)
        state_out[:, at : at + 256] = mm(b_t, ve).astype(BF16)


def col_table(pair, course):
    shape = (384, 256)
    return as_bf16((iota(shape, 0) & 127) == course * 32 + 2 * pair + (iota(shape, 1) >> 7))


def step_table(pair, course):
    shape = (256, 128)
    return as_bf16((iota(shape, 0) & 127) == 64 + course * 32 + 2 * pair + (iota(shape, 1) >> 6))


def halves(value):
    lane = iota(value.shape, 1)
    zero = jnp.zeros_like(value)
    return jnp.where(lane < 64, value, zero), jnp.where(lane >= 64, value, zero)


def within_kernel(ksp, kt, bc, xh, y0, y1, gram):
    pair = pl.program_id(0)
    half = bc.shape[0] // 2

    @pl.when(pair == 0)
    def _():
        shape = (2 * half, 2 * half)
        row, col = iota(shape, 0), iota(shape, 1)
        for course in range(2):
            value = mm_nt(bc[:, 256 * course + 128 : 256 * course + 256], bc[:, 256 * course : 256 * course + 128])
            gram[course] = jnp.where(col <= row if course == 0 else col >= row, value, 0.0)

    x = xh[...].astype(F32)
    for course, out in ((0, y0), (1, y1)):
        cols = mm(ksp[...], col_table(pair, course))
        v = (x * mm(ksp[:, :256], step_table(pair, course))).astype(BF16)
        v_a, v_b = halves(v)
        for tb in range(2):
            t_at = slice(tb * half, (tb + 1) * half)
            weights, values = [], []
            for sb in (range(tb + 1) if course == 0 else range(tb, 2)):
                s_at = slice(sb * half, (sb + 1) * half)
                for head, v_head in ((0, v_a), (1, v_b)):
                    gap = cols[t_at, 128 * head : 128 * head + 128] - kt[course, 0, head : head + 1, s_at]
                    if tb == sb:
                        gap = jnp.minimum(gap, 0.0)
                    weights.append((jnp.exp2(gap) * gram[course, t_at, s_at]).astype(BF16))
                    values.append(v_head[s_at])
            out[t_at, :] = mm(jnp.concatenate(weights, axis=1), jnp.concatenate(values, axis=0))


def cross_kernel(sel, bc, fac, state, y0w, y1w, goal, y0, y1, stats, acc):
    step = pl.program_id(0)
    lanes = state.shape[1]
    rd = 1 - sel[1]
    c_rows = jnp.where(rd == 0, bc[:, 128:256], bc[:, 384:512])
    table = spread_table(2, rd * 32 + step * (lanes // 64), lanes)
    carried = mm(parts(fac[...], 2), table) * mm(c_rows, state[...])
    first = y0w[...] + jnp.where(rd == 0, carried, 0.0)
    second = y1w[...] + jnp.where(rd == 1, carried, 0.0)
    y0[...] = first
    y1[...] = second
    y = first + second
    t = goal[...].astype(F32)

    @pl.when(step == 0)
    def _():
        acc[...] = jnp.zeros_like(acc)

    for slot, value in enumerate((y * y, y * t, t * t)):
        total = value[:, :128]
        for at in range(128, lanes, 128):
            total = total + value[:, at : at + 128]
        acc[slot] += total

    @pl.when(step == pl.num_programs(0) - 1)
    def _():
        lane = iota(stats.shape, 1)
        out = jnp.zeros(stats.shape, F32)
        for slot in range(3):
            out = jnp.where(lane == slot, jnp.sum(acc[slot], axis=1, keepdims=True), out)
        stats[...] = out


def loss_kernel(sel, own, other, mask, bc, fac, y0, y1, goal, go_out, direct_out, *, count):
    step = pl.program_id(0)
    lanes = goal.shape[1]
    rd = 1 - sel[1]
    stats = (own[...] + other[...]) * (1.0 / count)
    ry = jnp.sqrt(stats[:, 0:1] + EPSILON)
    rt = jnp.sqrt(stats[:, 2:3] + EPSILON)
    cosine = stats[:, 1:2] / (ry * rt)
    masked = mask[...] > 0.0
    y_scale = jnp.where(masked, cosine / (ry * ry), 0.0)
    t_scale = jnp.where(masked, 1.0 / (rt * ry), 0.0)
    go = (y_scale * (y0[...] + y1[...]) - t_scale * goal[...].astype(F32)).astype(BF16)
    go_out[...] = go
    table = spread_table(2, rd * 32 + step * (lanes // 64), lanes)
    scaled = (mm(parts(fac[...], 2), table) * go.astype(F32)).astype(BF16)
    c_t = jnp.where(rd == 0, bc[:, 128:256], bc[:, 384:512]).astype(F32).T.astype(BF16)
    direct_out[...] = mm(c_t, scaled).astype(BF16)


def head_sums(products, bases, pair):
    stacked = jnp.concatenate([parts(product, 2) for product in products], axis=1)
    shape = (stacked.shape[1], 128)
    row, col = iota(shape, 0), iota(shape, 1)
    target = jnp.zeros(shape, jnp.int32)
    for index, base in enumerate(bases):
        target = jnp.where((row >> 8) == index, base, target)
    return mm(stacked, as_bf16(col == target + 2 * pair + ((row & 127) >> 6)))


def back_within_kernel(ksp, kt, bc, xh, go_ref, y0, y1, gx_out, sums_out, gbc_out, gram, grad_gram, sums):
    pair = pl.program_id(0)
    half = bc.shape[0] // 2

    @pl.when(pair == 0)
    def _():
        shape = (2 * half, 2 * half)
        row, col = iota(shape, 0), iota(shape, 1)
        for course in range(2):
            value = mm_nt(bc[:, 256 * course : 256 * course + 128], bc[:, 256 * course + 128 : 256 * course + 256])
            gram[course] = jnp.where(row <= col if course == 0 else row >= col, value, 0.0)
        grad_gram[...] = jnp.zeros_like(grad_gram)
        sums[...] = jnp.zeros_like(sums)

    x = xh[...].astype(F32)
    go = go_ref[...]
    go_f = go.astype(F32)
    go_a, go_b = halves(go)
    grad_x = jnp.zeros(x.shape, F32)
    products = []
    for course in range(2):
        cols = mm(ksp[...], col_table(pair, course))
        step = mm(ksp[:, :256], step_table(pair, course))
        v_a, v_b = halves((x * step).astype(BF16))
        grads = []
        for sb in range(2):
            s_at = slice(sb * half, (sb + 1) * half)
            weights, values = [], []
            for tb in (range(sb, 2) if course == 0 else range(sb + 1)):
                t_at = slice(tb * half, (tb + 1) * half)
                gained = None
                for head, v_head, go_head in ((0, v_a, go_a), (1, v_b, go_b)):
                    gap = kt[course, 0, head : head + 1, t_at] - cols[s_at, 128 * head : 128 * head + 128]
                    if tb == sb:
                        gap = jnp.minimum(gap, 0.0)
                    decay = jnp.exp2(gap)
                    weights.append((decay * gram[course, s_at, t_at]).astype(BF16))
                    values.append(go_head[t_at])
                    term = mm_nt(v_head[s_at], go[t_at]) * decay
                    gained = term if gained is None else gained + term
                grad_gram[course, s_at, t_at] += gained
            grads.append(mm(jnp.concatenate(weights, axis=1), jnp.concatenate(values, axis=0)))
        grad_v = jnp.concatenate(grads, axis=0)
        grad_x = grad_x + step * grad_v
        products.append(x * grad_v)
    gx_out[...] = grad_x
    products += [go_f * y0[...], go_f * y1[...]]
    sums[...] += head_sums(products, (0, 32, 64, 96), pair)

    @pl.when(pair == pl.num_programs(0) - 1)
    def _():
        sums_out[...] = sums[...]
        shape = (2 * half, 2 * half)
        row, col = iota(shape, 0), iota(shape, 1)
        for course in range(2):
            keep = row <= col if course == 0 else row >= col
            gg = jnp.where(keep, grad_gram[course], 0.0)
            at = 256 * course
            gbc_out[:, at : at + 128] = mm(gg.astype(BF16), bc[:, at + 128 : at + 256])
            gbc_out[:, at + 128 : at + 256] = mm(gg.T.astype(BF16), bc[:, at : at + 128])


def back_cross_kernel(
    sel, adjoint, state, bc, fac, ksp, z_ref, rate, xh, go_ref, gxw, sums_in, gbc_in, gx_out, grad_out, sums, grads
):
    step = pl.program_id(0)
    lanes = xh.shape[1]
    tokens = xh.shape[0]
    core, sd = sel[0], sel[1]
    rd = 1 - sd
    heads = lanes // 64

    @pl.when(step == 0)
    def _():
        sums[...] = jnp.zeros_like(sums)
        grads[...] = jnp.zeros_like(grads)

    factors = parts(fac[...], 2)
    leaving = mm(factors, spread_table(2, 64 + sd * 32 + step * heads, lanes))
    entering = mm(factors, spread_table(2, rd * 32 + step * heads, lanes))
    size = mm(ksp[:, :256], spread_table(2, 64 + sd * 32 + step * heads, lanes))
    x = xh[...].astype(F32)
    b_rows = jnp.where(sd == 0, bc[:, :128], bc[:, 256:384])
    grad_v = mm(b_rows, adjoint[...]) * leaving
    gx_out[...] = (gxw[...] + size * grad_v).astype(BF16)
    product = x * grad_v
    shape = (2 * lanes, 128)
    row, col = iota(shape, 0), iota(shape, 1)
    target = sd * 32 + step * heads + ((row & (lanes - 1)) >> 6)
    sums[...] += mm(parts(product, 2), as_bf16(col == target))
    ve = (x * size * leaving).astype(BF16)
    grads[0] += mm_nt(ve, adjoint[...])
    scaled = (entering * go_ref[...].astype(F32)).astype(BF16)
    grads[1] += mm_nt(scaled, state[...])

    @pl.when(step == pl.num_programs(0) - 1)
    def _():
        within = sums_in[...]
        cross = sums[...]
        size4 = ksp[:, :128].astype(F32) + ksp[:, 128:256].astype(F32) + ksp[:, 256:].astype(F32)
        lane = iota((tokens, 128), 1)
        size4 = jnp.where(lane < 64, pltpu.roll(size4, 64, 1), size4)
        moved = pltpu.roll(within, 64, 1)
        rs = within + cross
        grad_k = moved - size4 * rs
        r_total = jnp.sum(size4 * cross, axis=0, keepdims=True)
        trow, tcol = iota((tokens, tokens), 0), iota((tokens, tokens), 1)
        later = exact_sum(as_bf16(tcol >= trow), grad_k)
        earlier = exact_sum(as_bf16(tcol <= trow), grad_k)
        grad_g = jnp.where(lane < 32, later, earlier) + r_total
        sigma = 1.0 / (1.0 + jnp.exp(-z_ref[...]))
        grad_z = jnp.where(lane < 64, (rs - rate[...] * grad_g) * sigma, 0.0)

        def place(row_at, col_at):
            return (row_at < 64) & (col_at == ((row_at >> 5) & 1) * 64 + core * 32 + (row_at & 31))

        grad_out[:, 512:640] = pick(grad_z, place, 3)
        gbc = gbc_in[...]
        grad_out[:, 0:128] = gbc[:, 0:128] + jnp.where(sd == 0, grads[0], 0.0)
        grad_out[:, 128:256] = gbc[:, 128:256] + jnp.where(rd == 0, grads[1], 0.0)
        grad_out[:, 256:384] = gbc[:, 256:384] + jnp.where(sd == 1, grads[0], 0.0)
        grad_out[:, 384:512] = gbc[:, 384:512] + jnp.where(rd == 1, grads[1], 0.0)


def shaped(shape, dtype):
    return jax.ShapeDtypeStruct(shape, dtype)


SMEM = pl.BlockSpec(memory_space=pltpu.SMEM)


def whole(array):
    rank = len(array.shape)
    return pl.BlockSpec(array.shape, lambda *_: (0,) * rank)


def lanes_block(rows, lanes):
    return pl.BlockSpec((rows, lanes), lambda i: (0, i))


def call(body, grid, in_specs, out_specs, out_shape, scratch=()):
    return pl.pallas_call(
        body,
        grid=grid,
        in_specs=in_specs,
        out_specs=out_specs,
        out_shape=out_shape,
        scratch_shapes=list(scratch),
        compiler_params=pltpu.CompilerParams(vmem_limit_bytes=VMEM_LIMIT),
    )


def ring(count, distance):
    return [(i, (i + distance) % count) for i in range(count)]


def swapped(value, axis):
    return lax.ppermute(value, axis, [(0, 1), (1, 0)])


def ordered(core, own, other, axis=0):
    return jnp.where(
        core == 0, jnp.concatenate([own, other], axis=axis), jnp.concatenate([other, own], axis=axis)
    )


def gather_weight(weight, sizes):
    nz, nx, nyh = sizes
    half = nz // 2
    slots = []
    for i in range(half):
        route = []
        for z in range(nz):
            route.append((2 * z, 2 * ((z + half - 1 - i) % nz)))
            route.append((2 * z + 1, 2 * ((z - i - 1) % nz) + 1))
        slots.append(lax.ppermute(weight, ("z", "c"), route))
    first = jnp.concatenate(slots[: half // 2], axis=0)
    second = jnp.concatenate(slots[half // 2 :], axis=0)
    first = jnp.concatenate([first, swapped(first, "yh")], axis=0)
    second = jnp.concatenate([second] + [lax.ppermute(second, "x", ring(nx, k)) for k in range(1, nx)], axis=0)
    first = jnp.concatenate([first] + [lax.ppermute(first, "x", ring(nx, k)) for k in range(1, nx)], axis=0)
    second = jnp.concatenate([second, swapped(second, "yh")], axis=0)
    return first, second


def relative_tables(sizes, rows, slots):
    nz, nx, nyh = sizes
    x, yh = lax.axis_index("x"), lax.axis_index("yh")
    block = nx * nyh * rows
    count = slots * block
    src = jnp.arange(count)[:, None]
    dst = jnp.arange(count)[None, :]
    r, rest = dst % rows, dst // rows
    slot, rest = rest % slots, rest // slots
    tables = []
    for x_first in (True, False):
        if x_first:
            yr, xr = rest % nyh, rest // nyh
        else:
            xr, yr = rest % nx, rest // nx
        source = slot * block + (((x - xr) % nx) * nyh + (yh + yr) % nyh) * rows + r
        tables.append((src == source).astype(BF16))
    return tables


def quarter_table(sizes, rows):
    nz, nx, nyh = sizes
    x = lax.axis_index("x")
    block = nx * nyh * rows
    quarter = rows // 4
    src = jnp.arange(block)[:, None]
    dst = jnp.arange(block)[None, :]
    r, rest = dst % quarter, dst // quarter
    yh, rest = rest % nyh, rest // nyh
    xr, q = rest % nx, rest // nx
    source = (((x + xr) % nx) * nyh + yh) * rows + q * quarter + r
    return (src == source).astype(BF16)


def moved(value, table):
    return jnp.dot(value, table, preferred_element_type=F32).astype(BF16)


def shards(sizes, layer_input, head_input, targets, proj_weight, rates, dt_bias, mask_index):
    nz, nx, nyh = sizes
    z, x, yh = (lax.axis_index(name) for name in ("z", "x", "yh"))
    yl, core = lax.axis_index("yl"), lax.axis_index("c")
    tokens, depth = layer_input.shape
    features = head_input.shape[1]
    wide = features // 2
    rows, columns = proj_weight.shape
    chip = 2 * tokens
    pairs = wide // 128
    half = nz // 2
    slots = half // 2
    block = depth // nz
    quarter = rows // 4

    part_a, part_b = gather_weight(proj_weight, sizes)

    def own_heads(array):
        parts_of = array.reshape(tokens, 2, wide)
        mine = lax.dynamic_index_in_dim(parts_of, core, 1, keepdims=False)
        theirs = lax.dynamic_index_in_dim(parts_of, 1 - core, 1, keepdims=False)
        return ordered(core, mine, swapped(theirs, "c"))

    xh = own_heads(head_input)
    goal = own_heads(targets)

    start = (z - (half - 1)) % nz
    blocks = layer_input.reshape(tokens, nz, block)
    turned = lax.dynamic_slice_in_dim(jnp.concatenate([blocks, blocks], axis=1), start, nz, axis=1)
    turned = turned.reshape(tokens, 2, 2, slots * block)
    tables = relative_tables(sizes, rows, slots)
    ranked = jnp.stack([moved(turned[:, :, i], tables[i]) for i in range(2)], axis=2)
    mine = lax.dynamic_index_in_dim(ranked, core, 1, keepdims=False).reshape(tokens, -1)
    theirs = lax.dynamic_index_in_dim(ranked, 1 - core, 1, keepdims=False).reshape(tokens, -1)
    chip_input = ordered(core, mine, swapped(theirs, "c"))
    span = slots * block

    place = quarter_table(sizes, rows)
    by_quarter = moved(blocks, place).reshape(tokens, nz, 4, block // 4)
    by_quarter = jnp.transpose(by_quarter, (2, 0, 1, 3)).reshape(4, tokens, depth // 4)
    member = 2 * yl + core
    group = [lax.dynamic_index_in_dim(by_quarter, member, 0, keepdims=False)]
    for k in (1, 2, 3):
        sent = lax.dynamic_index_in_dim(by_quarter, member ^ k, 0, keepdims=False)
        group.append(lax.ppermute(sent, SEQ, [(i, i ^ k) for i in range(4)]))
    group_input = jnp.concatenate(group, axis=0)

    positions = yl * chip + jnp.arange(chip, dtype=jnp.int32)
    mask = jnp.any(positions[:, None] == mask_index[0][None, :], axis=1).astype(F32)[:, None]

    def by_core(table):
        own = lax.dynamic_slice_in_dim(table, core * 32, 32, axis=1).reshape(1, 64)
        return jnp.concatenate([own, own], axis=1)

    bias4, rate4 = by_core(dt_bias), by_core(rates)
    sel = jnp.stack([core, yl]).astype(jnp.int32)

    projected = jnp.dot(chip_input[:, :span], part_a, preferred_element_type=F32) + jnp.dot(
        chip_input[:, span:], part_b, preferred_element_type=F32
    )
    projected_other = swapped(projected, "c")

    outs = [
        shaped((chip, 512), BF16),
        shaped((chip, 384), BF16),
        shaped((128, chip), F32),
        shaped((chip, 128), F32),
        shaped((chip, 128), F32),
        shaped((128, wide), BF16),
    ]
    ins = [projected, projected_other, xh, bias4, rate4]
    bc, ksp, kt, fac, z4, leaving = call(
        prepare_kernel, (), [SMEM] + [whole(a) for a in ins], [whole(a) for a in outs], outs
    )(sel, *ins)
    entering = swapped(leaving, "yl")

    kt4 = kt[:64].reshape(2, pairs, 2, chip)
    kt_spec = pl.BlockSpec((2, 1, 2, chip), lambda i: (0, i, 0, 0))
    pair_spec = lanes_block(chip, 128)
    wide_f32 = shaped((chip, wide), F32)
    y0w, y1w = call(
        within_kernel,
        (pairs,),
        [whole(ksp), kt_spec, whole(bc), pair_spec],
        [pair_spec] * 2,
        [wide_f32] * 2,
        [pltpu.VMEM((2, chip, chip), F32)],
    )(ksp, kt4, bc, xh)

    lanes = 512
    steps = wide // lanes
    big = lanes_block(chip, lanes)
    state_spec = lanes_block(128, lanes)
    stats_shape = shaped((chip, 128), F32)
    y0, y1, stats = call(
        cross_kernel,
        (steps,),
        [SMEM, whole(bc), whole(fac), state_spec, big, big, big],
        [big, big, whole(stats_shape)],
        [wide_f32, wide_f32, stats_shape],
        [pltpu.VMEM((3, chip, 128), F32)],
    )(sel, bc, fac, entering, y0w, y1w, goal)
    stats_other = swapped(stats, "c")

    def loss_body(*refs):
        loss_kernel(*refs, count=features)

    go, direct = call(
        loss_body,
        (steps,),
        [SMEM, whole(stats), whole(stats), whole(mask), whole(bc), whole(fac), big, big, big],
        [big, state_spec],
        [shaped((chip, wide), BF16), shaped((128, wide), BF16)],
    )(sel, stats, stats_other, mask, bc, fac, y0, y1, goal)
    adjoint = swapped(direct, "yl")

    gbc_shape = shaped((chip, 512), F32)
    gxw, sums, gbc = call(
        back_within_kernel,
        (pairs,),
        [whole(ksp), kt_spec, whole(bc)] + [pair_spec] * 4,
        [pair_spec, whole(stats_shape), whole(gbc_shape)],
        [wide_f32, stats_shape, gbc_shape],
        [pltpu.VMEM((2, chip, chip), F32), pltpu.VMEM((2, chip, chip), F32), pltpu.VMEM((chip, 128), F32)],
    )(ksp, kt4, bc, xh, go, y0, y1)

    grad_shape = shaped((chip, columns), F32)
    gx, grad = call(
        back_cross_kernel,
        (steps,),
        [SMEM, state_spec, state_spec]
        + [whole(a) for a in (bc, fac, ksp, z4, rate4)]
        + [big, big, big, whole(sums), whole(gbc)],
        [big, whole(grad_shape)],
        [shaped((chip, wide), BF16), grad_shape],
        [pltpu.VMEM((chip, 128), F32), pltpu.VMEM((2, chip, 128), F32)],
    )(sel, adjoint, entering, bc, fac, ksp, z4, rate4, xh, go, gxw, sums, gbc)

    grad_proj = (grad + swapped(grad, "c")).astype(BF16)
    grad_proj = jnp.where(
        core == 0, grad_proj, jnp.concatenate([grad_proj[tokens:], grad_proj[:tokens]], axis=0)
    )
    grad_group = jnp.concatenate([grad_proj, swapped(grad_proj, "yl")], axis=0)
    grad_rows = lax.dot_general(
        group_input, grad_group, (((0,), (0,)), ((), ())), preferred_element_type=F32
    ).astype(BF16)
    grad_rows = grad_rows.reshape(nz, nx, nyh * quarter, columns)
    total = grad_rows[:, 0].astype(F32)
    for k in range(1, nx):
        total = total + lax.ppermute(grad_rows[:, k], "x", ring(nx, k)).astype(F32)
    total = total.astype(BF16).reshape(nz * nyh, quarter, columns)
    total = lax.all_to_all(total, ("z", "yh"), 0, 0, tiled=True)
    total = jnp.sum(total.astype(F32), axis=0)
    grad_weight = lax.all_gather(total, SEQ, axis=0, tiled=True)

    gx2 = gx.reshape(2, tokens, wide)
    gx_mine = lax.dynamic_index_in_dim(gx2, core, 0, keepdims=False)
    gx_theirs = lax.dynamic_index_in_dim(gx2, 1 - core, 0, keepdims=False)
    grad_x = ordered(core, gx_mine, swapped(gx_theirs, "c"), axis=1)

    wide_grad = jnp.concatenate(
        [
            lax.dot_general(grad_proj, part, (((1,), (1,)), ((), ())), preferred_element_type=F32).astype(BF16)
            for part in (part_a, part_b)
        ],
        axis=1,
    )
    full = ordered(core, wide_grad[:tokens], swapped(wide_grad[tokens:], "c"), axis=1)
    full = full.reshape(tokens, 2, 2, span)
    back = jnp.stack([moved(full[:, :, i], tables[i].T) for i in range(2)], axis=2).reshape(tokens, nz, block)
    grad_input = lax.dynamic_slice_in_dim(
        jnp.concatenate([back, back], axis=1), (nz - start) % nz, nz, axis=1
    ).reshape(tokens, depth)
    return grad_x, grad_input, grad_weight


def solution(mesh):
    sizes = fsdp_axes(mesh.shape["fsdp"])
    fine = Mesh(np.asarray(mesh.devices).reshape(*sizes, 2, 2), ("z", "x", "yh", "yl", "c"))
    fsdp = ("z", "x", "yh")
    tokens = P(fsdp + SEQ, None)
    rows = P(fsdp, None)

    def body(*arrays):
        return shards(sizes, *arrays)

    return jax.shard_map(
        body,
        mesh=fine,
        in_specs=(tokens, tokens, tokens, rows, P(), P(), rows),
        out_specs=(tokens, tokens, rows),
        check_vma=False,
    )
```

```python
import jax
import jax.numpy as jnp
import numpy as np
from jax import lax
from jax.experimental import pallas as pl
from jax.experimental.pallas import tpu as pltpu
from jax.sharding import Mesh
from jax.sharding import PartitionSpec as P

EPSILON = 1e-06
LOG2E = 1.4426950408889634
F32 = jnp.float32
BF16 = jnp.bfloat16
SEQ = ("yl", "c")
VMEM_LIMIT = 24 * 1024 * 1024
GROUP = 8


def fsdp_axes(count):
    return (count // 8, 4, 2)


def iota(shape, dim):
    return lax.broadcasted_iota(jnp.int32, shape, dim)


def mm(left, right):
    return lax.dot_general(left, right, (((1,), (0,)), ((), ())), preferred_element_type=F32)


def mm_nt(left, right):
    return lax.dot_general(left, right, (((1,), (1,)), ((), ())), preferred_element_type=F32)


def parts(value, count):
    pieces = []
    for _ in range(count):
        piece = value.astype(BF16)
        pieces.append(piece)
        value = value - piece.astype(F32)
    return jnp.concatenate(pieces, axis=1)


def as_bf16(condition):
    return jnp.where(condition, 1.0, 0.0).astype(BF16)


def exact_sum(mask, value):
    width = value.shape[1]
    out = mm(mask, parts(value, 3))
    return out[:, :width] + out[:, width : 2 * width] + out[:, 2 * width :]


def pick(value, chosen, pieces):
    rows, width = value.shape
    table = as_bf16(chosen(iota((pieces * width, width), 0) & (width - 1), iota((pieces * width, width), 1)))
    return mm(parts(value, pieces), table)


def spread_table(pieces, lane_base, lanes):
    shape = (pieces * 128, lanes)
    return as_bf16((iota(shape, 0) & 127) == lane_base + (iota(shape, 1) >> 6))


def block_at(z, core, i, count):
    half = count // 2
    return (jnp.where(core == 0, z + count - (half - 1 - i), z + i + 1)) & (count - 1)


def rank_kernel(sel, rows_in, mine, theirs, *quarters, sizes):
    nz, nx, nyh = sizes
    core, member, z, x, yh = sel[0], sel[2], sel[3], sel[4], sel[5]
    tokens = rows_in.shape[0]
    block = 128 * nx
    low_lanes = iota((tokens, 128), 1) < 64
    for out, owner in ((mine, core), (theirs, 1 - core)):
        for part in range(2):
            starts = [block_at(z, owner, 2 * part + i, nz) * block for i in range(2)]
            for xr in range(nx):
                at = ((x + nx - xr) & (nx - 1)) * 128
                tiles = [rows_in[:, pl.ds(pl.multiple_of(start + at, 128), 128)].astype(F32) for start in starts]
                low = jnp.where(low_lanes, tiles[0], pltpu.roll(tiles[1], 64, 1))
                high = jnp.where(low_lanes, pltpu.roll(tiles[0], 64, 1), tiles[1])
                for yr in range(nyh):
                    place = (xr * nyh + yr) if part == 0 else (yr * nx + xr)
                    to = part * 2 * block + place * 128
                    out[:, to : to + 128] = jnp.where(yh == yr, low, high).astype(BF16)
    dst = iota((1, block), 1)
    xr, yr = (dst >> 5) & (nx - 1), (dst >> 4) & 1
    source = ((x + xr) & (nx - 1)) * 128 + (yh ^ yr) * 64 + (member ^ (dst >> 7)) * 16 + (dst & 15)
    table = as_bf16(iota((block, block), 0) == source)
    for zz in range(nz):
        value = mm(rows_in[:, zz * block : (zz + 1) * block], table).astype(BF16)
        for k, out in enumerate(quarters):
            out[:, zz * 128 : (zz + 1) * 128] = value[:, k * 128 : (k + 1) * 128]


def unrank_kernel(sel, mine, theirs, out, *, sizes):
    nz, nx, nyh = sizes
    core, z, x, yh = sel[0], sel[3], sel[4], sel[5]
    tokens = out.shape[0]
    block = 128 * nx
    low_lanes = iota((tokens, 128), 1) < 64
    for ref, owner in ((mine, core), (theirs, 1 - core)):
        for part in range(2):
            starts = [block_at(z, owner, 2 * part + i, nz) * block for i in range(2)]
            for xr in range(nx):
                at = ((x + nx - xr) & (nx - 1)) * 128
                pair = []
                for yr in range(nyh):
                    place = (xr * nyh + yr) if part == 0 else (yr * nx + xr)
                    to = part * 2 * block + place * 128
                    pair.append(ref[:, to : to + 128].astype(F32))
                low = jnp.where(yh == 0, pair[0], pair[1])
                high = jnp.where(yh == 0, pair[1], pair[0])
                first = jnp.where(low_lanes, low, pltpu.roll(high, 64, 1))
                second = jnp.where(low_lanes, pltpu.roll(low, 64, 1), high)
                for start, tile in zip(starts, (first, second)):
                    out[:, pl.ds(pl.multiple_of(start + at, 128), 128)] = tile.astype(BF16)


def prepare_kernel(sel, pa, pb, xlo, xhi, bias, rate, bc_out, ksp_out, kj_out, kt_out, fac_out, z_out, state_out):
    tokens = pa.shape[0]
    core, sd = sel[0], sel[1]
    proj = pa[...] + pb[...]
    bc = proj[:, :512].astype(BF16)
    bc_out[...] = bc

    def source(row, col):
        return row == ((col >> 5) & 1) * 64 + core * 32 + (col & 31)

    z = pick(proj[:, 512:640], source, 3) + bias[...]
    z_out[...] = z
    step = jnp.maximum(z, 0.0) + jnp.log1p(jnp.exp(-jnp.abs(z)))
    g = -rate[...] * step * LOG2E
    row = iota((tokens, tokens), 0)
    col = iota((tokens, tokens), 1)
    low = exact_sum(as_bf16(col <= row), g)
    high = exact_sum(as_bf16(col >= row), g)
    lane = iota((tokens, 128), 1)
    first = ((lane >> 5) & 1) == 0
    k = jnp.where(first, low, high)
    total = jnp.where(first[:1], low[tokens - 1 :], high[:1])
    ks = jnp.where(lane < 64, k, step)
    ksp_out[...] = parts(ks, 3)
    kt_out[...] = ks.T
    for at in range(kj_out.shape[0]):
        kj_out[at] = ks if at == 0 else pltpu.roll(ks, 128 - GROUP * at, 1)
    leaving = jnp.exp2(total - k)
    fac_out[...] = jnp.where(lane < 64, jnp.exp2(k), leaving)
    factor = parts(step * leaving, 2)
    b_t = jnp.where(sd == 0, proj[:, :128], proj[:, 256:384]).T.astype(BF16)
    width = xlo.shape[1]
    for at in range(0, width, 256):
        table = spread_table(2, sd * 32 + at // 64, 256)
        x = jnp.concatenate([xlo[:, at : at + 256], xhi[:, at : at + 256]], axis=0)
        ve = (x.astype(F32) * mm(factor, table)).astype(BF16)
        state_out[:, at : at + 256] = mm(b_t, ve).astype(BF16)


def halves(value):
    first = (iota(value.shape, 1) & 64) == 0
    zero = jnp.zeros_like(value)
    return jnp.where(first, value, zero), jnp.where(first, zero, value)


def set_up(gram, tables, bc, lanes, transposed):
    half = bc.shape[0] // 2
    shape = (2 * half, 2 * half)
    row, col = iota(shape, 0), iota(shape, 1)
    for course in range(2):
        b_rows = bc[:, 256 * course : 256 * course + 128]
        c_rows = bc[:, 256 * course + 128 : 256 * course + 256]
        value = mm_nt(b_rows, c_rows) if transposed else mm_nt(c_rows, b_rows)
        keep = col <= row if (course == 0) != transposed else col >= row
        gram[course] = jnp.where(keep, value, 0.0)
        tables[course] = spread_table(2, 64 + 32 * course, lanes)


def within_kernel(sel, kj, kt, bc, xlo, xhi, y_sd, y_rd, gram, tables):
    half = bc.shape[0] // 2
    sd = sel[1]

    @pl.when(pl.program_id(0) == 0)
    def _():
        set_up(gram, tables, bc, xlo.shape[1], False)

    x = jnp.concatenate([xlo[...], xhi[...]], axis=0).astype(F32)
    ks = kj[0]
    ks_parts = parts(ks, 2)
    results = []
    for course in range(2):
        v_a, v_b = halves((x * mm(ks_parts, tables[course])).astype(BF16))
        by_rows = []
        for tb in range(2):
            t_at = slice(tb * half, (tb + 1) * half)
            sources = range(tb + 1) if course == 0 else range(tb, 2)
            weights = [[] for _ in range(GROUP // 2)]
            values = [[] for _ in range(GROUP // 2)]
            for sb in sources:
                s_at = slice(sb * half, (sb + 1) * half)
                table = gram[course, t_at, s_at]
                for head in range(GROUP):
                    lane = 32 * course + head
                    gap = ks[t_at, lane : lane + 1] - kt[course, 0, head : head + 1, s_at]
                    if tb == sb:
                        gap = jnp.minimum(gap, 0.0)
                    pair = head // 2
                    weights[pair].append((jnp.exp2(gap) * table).astype(BF16))
                    values[pair].append((v_a, v_b)[head % 2][s_at, 128 * pair : 128 * pair + 128])
            by_rows.append(
                jnp.concatenate(
                    [
                        mm(jnp.concatenate(w, axis=1), jnp.concatenate(v, axis=0))
                        for w, v in zip(weights, values)
                    ],
                    axis=1,
                )
            )
        results.append(jnp.concatenate(by_rows, axis=0))
    y_sd[...] = jnp.where(sd == 0, results[0], results[1]).astype(BF16)
    y_rd[...] = jnp.where(sd == 0, results[1], results[0]).astype(BF16)


def cross_kernel(sel, bc, fac, state, y_sd, y_rd, glo, ghi, y_out, stats, acc):
    step = pl.program_id(0)
    lanes = state.shape[1]
    rd = 1 - sel[1]
    c_rows = jnp.where(rd == 0, bc[:, 128:256], bc[:, 384:512])
    table = spread_table(2, rd * 32 + step * (lanes // 64), lanes)
    carried = mm(parts(fac[...], 2), table) * mm(c_rows, state[...])
    y = y_sd[...].astype(F32) + y_rd[...].astype(F32) + carried
    y_out[...] = y.astype(BF16)
    t = jnp.concatenate([glo[...], ghi[...]], axis=0).astype(F32)

    @pl.when(step == 0)
    def _():
        acc[...] = jnp.zeros_like(acc)

    for slot, value in enumerate((y * y, y * t, t * t)):
        total = value[:, :128]
        for at in range(128, lanes, 128):
            total = total + value[:, at : at + 128]
        acc[slot] += total

    @pl.when(step == pl.num_programs(0) - 1)
    def _():
        lane = iota(stats.shape, 1)
        out = jnp.zeros(stats.shape, F32)
        for slot in range(3):
            out = jnp.where(lane == slot, jnp.sum(acc[slot], axis=1, keepdims=True), out)
        stats[...] = out


def loss_kernel(sel, own, other, mask, bc, fac, y_ref, glo, ghi, go_out, direct_out, *, count):
    step = pl.program_id(0)
    lanes = glo.shape[1]
    rd = 1 - sel[1]
    stats = (own[...] + other[...]) * (1.0 / count)
    ry = jnp.sqrt(stats[:, 0:1] + EPSILON)
    rt = jnp.sqrt(stats[:, 2:3] + EPSILON)
    cosine = stats[:, 1:2] / (ry * rt)
    masked = mask[...] > 0.0
    y_scale = jnp.where(masked, cosine / (ry * ry), 0.0)
    t_scale = jnp.where(masked, 1.0 / (rt * ry), 0.0)
    t = jnp.concatenate([glo[...], ghi[...]], axis=0).astype(F32)
    go = (y_scale * y_ref[...].astype(F32) - t_scale * t).astype(BF16)
    go_out[...] = go
    table = spread_table(2, rd * 32 + step * (lanes // 64), lanes)
    scaled = (mm(parts(fac[...], 2), table) * go.astype(F32)).astype(BF16)
    c_t = jnp.where(rd == 0, bc[:, 128:256], bc[:, 384:512]).astype(F32).T.astype(BF16)
    direct_out[...] = mm(c_t, scaled).astype(BF16)


def back_within_kernel(
    sel, kj, kt, bc, xlo, xhi, go_ref, y_ref, y_sd, gx_out, sums_out, gbc_out, gram, tables, grad_gram, sums, place
):
    half = bc.shape[0] // 2
    step_at = pl.program_id(0)
    lanes = xlo.shape[1]
    sd = sel[1]

    @pl.when(step_at == 0)
    def _():
        set_up(gram, tables, bc, lanes, True)
        shape = (4 * lanes, 128)
        row, col = iota(shape, 0), iota(shape, 1)
        place[...] = as_bf16(col == (row // lanes) * 32 + ((row & (lanes - 1)) >> 6))
        grad_gram[...] = jnp.zeros_like(grad_gram)
        sums[...] = jnp.zeros_like(sums)

    x = jnp.concatenate([xlo[...], xhi[...]], axis=0).astype(F32)
    go = go_ref[...]
    go_f = go.astype(F32)
    go_heads = halves(go)
    ks = kj[0]
    ks_parts = parts(ks, 2)
    grad_x = None
    products = []
    for course in range(2):
        step = mm(ks_parts, tables[course])
        v_heads = halves((x * step).astype(BF16))
        by_rows = []
        for sb in range(2):
            s_at = slice(sb * half, (sb + 1) * half)
            weights = [[] for _ in range(GROUP // 2)]
            values = [[] for _ in range(GROUP // 2)]
            for tb in (range(sb, 2) if course == 0 else range(sb + 1)):
                t_at = slice(tb * half, (tb + 1) * half)
                table = gram[course, s_at, t_at]
                gained = None
                for head in range(GROUP):
                    pair = head // 2
                    pair_at = slice(128 * pair, 128 * pair + 128)
                    lane = 32 * course + head
                    gap = kt[course, 0, head : head + 1, t_at] - ks[s_at, lane : lane + 1]
                    if tb == sb:
                        gap = jnp.minimum(gap, 0.0)
                    decay = jnp.exp2(gap)
                    weights[pair].append((decay * table).astype(BF16))
                    values[pair].append(go_heads[head % 2][t_at, pair_at])
                    term = mm_nt(v_heads[head % 2][s_at, pair_at], go[t_at, pair_at]) * decay
                    gained = term if gained is None else gained + term
                grad_gram[course, s_at, t_at] += gained
            by_rows.append(
                jnp.concatenate(
                    [
                        mm(jnp.concatenate(w, axis=1), jnp.concatenate(v, axis=0))
                        for w, v in zip(weights, values)
                    ],
                    axis=1,
                )
            )
        grad_v = jnp.concatenate(by_rows, axis=0)
        part = step * grad_v
        grad_x = part if grad_x is None else grad_x + part
        products.append((x * grad_v).astype(BF16))
    gx_out[...] = grad_x.astype(BF16)
    own = y_sd[...].astype(F32)
    rest = y_ref[...].astype(F32) - own
    products.append((go_f * jnp.where(sd == 0, own, rest)).astype(BF16))
    products.append((go_f * jnp.where(sd == 0, rest, own)).astype(BF16))
    gained = mm(jnp.concatenate(products, axis=1), place[...])
    sums[...] += pltpu.roll(gained, GROUP * step_at, 1)

    @pl.when(step_at == pl.num_programs(0) - 1)
    def _():
        sums_out[...] = sums[...]
        shape = (2 * half, 2 * half)
        row, col = iota(shape, 0), iota(shape, 1)
        for course in range(2):
            keep = row <= col if course == 0 else row >= col
            gg = jnp.where(keep, grad_gram[course], 0.0)
            at = 256 * course
            gbc_out[:, at : at + 128] = mm(gg.astype(BF16), bc[:, at + 128 : at + 256])
            gbc_out[:, at + 128 : at + 256] = mm(gg.T.astype(BF16), bc[:, at : at + 128])


def back_cross_kernel(
    sel, adjoint, state, bc, fac, ksp, z_ref, rate, xlo, xhi, go_ref, gxw, sums_in, gbc_in, gx_out, grad_out, sums, grads
):
    step = pl.program_id(0)
    lanes = xlo.shape[1]
    tokens = bc.shape[0]
    core, sd = sel[0], sel[1]
    rd = 1 - sd
    heads = lanes // 64

    @pl.when(step == 0)
    def _():
        sums[...] = jnp.zeros_like(sums)
        grads[...] = jnp.zeros_like(grads)

    factors = parts(fac[...], 2)
    leaving = mm(factors, spread_table(2, 64 + sd * 32 + step * heads, lanes))
    entering = mm(factors, spread_table(2, rd * 32 + step * heads, lanes))
    size = mm(ksp[:, :256], spread_table(2, 64 + sd * 32 + step * heads, lanes))
    x = jnp.concatenate([xlo[...], xhi[...]], axis=0).astype(F32)
    b_rows = jnp.where(sd == 0, bc[:, :128], bc[:, 256:384])
    grad_v = mm(b_rows, adjoint[...]) * leaving
    gx_out[...] = (gxw[...].astype(F32) + size * grad_v).astype(BF16)
    product = x * grad_v
    shape = (2 * lanes, 128)
    row, col = iota(shape, 0), iota(shape, 1)
    target = sd * 32 + step * heads + ((row & (lanes - 1)) >> 6)
    sums[...] += mm(parts(product, 2), as_bf16(col == target))
    ve = (x * size * leaving).astype(BF16)
    grads[0] += mm_nt(ve, adjoint[...])
    scaled = (entering * go_ref[...].astype(F32)).astype(BF16)
    grads[1] += mm_nt(scaled, state[...])

    @pl.when(step == pl.num_programs(0) - 1)
    def _():
        within = sums_in[...]
        cross = sums[...]
        size4 = ksp[:, :128].astype(F32) + ksp[:, 128:256].astype(F32) + ksp[:, 256:].astype(F32)
        lane = iota((tokens, 128), 1)
        size4 = jnp.where(lane < 64, pltpu.roll(size4, 64, 1), size4)
        moved = pltpu.roll(within, 64, 1)
        rs = within + cross
        grad_k = moved - size4 * rs
        r_total = jnp.sum(size4 * cross, axis=0, keepdims=True)
        trow, tcol = iota((tokens, tokens), 0), iota((tokens, tokens), 1)
        later = exact_sum(as_bf16(tcol >= trow), grad_k)
        earlier = exact_sum(as_bf16(tcol <= trow), grad_k)
        grad_g = jnp.where(lane < 32, later, earlier) + r_total
        sigma = 1.0 / (1.0 + jnp.exp(-z_ref[...]))
        grad_z = jnp.where(lane < 64, (rs - rate[...] * grad_g) * sigma, 0.0)

        def place(row_at, col_at):
            return (row_at < 64) & (col_at == ((row_at >> 5) & 1) * 64 + core * 32 + (row_at & 31))

        grad_out[:, 512:640] = pick(grad_z, place, 3)
        gbc = gbc_in[...]
        grad_out[:, 0:128] = gbc[:, 0:128] + jnp.where(sd == 0, grads[0], 0.0)
        grad_out[:, 128:256] = gbc[:, 128:256] + jnp.where(rd == 0, grads[1], 0.0)
        grad_out[:, 256:384] = gbc[:, 256:384] + jnp.where(sd == 1, grads[0], 0.0)
        grad_out[:, 384:512] = gbc[:, 384:512] + jnp.where(rd == 1, grads[1], 0.0)


def shaped(shape, dtype):
    return jax.ShapeDtypeStruct(shape, dtype)


SMEM = pl.BlockSpec(memory_space=pltpu.SMEM)


def whole(array):
    rank = len(array.shape)
    return pl.BlockSpec(array.shape, lambda *_: (0,) * rank)


def lanes_block(rows, lanes):
    return pl.BlockSpec((rows, lanes), lambda i: (0, i))


def call(body, grid, in_specs, out_specs, out_shape, scratch=()):
    return pl.pallas_call(
        body,
        grid=grid,
        in_specs=in_specs,
        out_specs=out_specs,
        out_shape=out_shape,
        scratch_shapes=list(scratch),
        compiler_params=pltpu.CompilerParams(vmem_limit_bytes=VMEM_LIMIT),
    )


def ring(count, distance):
    return [(i, (i + distance) % count) for i in range(count)]


def swapped(value, axis):
    return lax.ppermute(value, axis, [(0, 1), (1, 0)])


def gather_along_z(weight, count):
    half = count // 2
    slots = []
    for i in range(half):
        route = []
        for z in range(count):
            route.append((2 * z, 2 * ((z + half - 1 - i) % count)))
            route.append((2 * z + 1, 2 * ((z - i - 1) % count) + 1))
        slots.append(lax.ppermute(weight, ("z", "c"), route))
    return slots


def with_x(value, count):
    return jnp.concatenate([value] + [lax.ppermute(value, "x", ring(count, k)) for k in range(1, count)], axis=0)


def with_yh(value):
    return jnp.concatenate([value, swapped(value, "yh")], axis=0)


def sum_over_x(value, count):
    total = value[:, 0].astype(F32)
    for k in range(1, count):
        total = total + lax.ppermute(value[:, k], "x", ring(count, k)).astype(F32)
    return total


def shards(sizes, layer_input, head_input, targets, proj_weight, rates, dt_bias, mask_index):
    nz, nx, nyh = sizes
    z, x, yh = (lax.axis_index(name) for name in ("z", "x", "yh"))
    yl, core = lax.axis_index("yl"), lax.axis_index("c")
    tokens, depth = layer_input.shape
    features = head_input.shape[1]
    wide = features // 2
    rows, columns = proj_weight.shape
    chip = 2 * tokens
    quarter = rows // 4
    sel = jnp.stack([core, yl, 2 * yl + core, z, x, yh]).astype(jnp.int32)

    slots = gather_along_z(proj_weight, nz)

    half_shape = shaped((tokens, depth // 2), BF16)
    quarter_shape = shaped((tokens, depth // 4), BF16)

    def rank_body(*refs):
        rank_kernel(*refs, sizes=sizes)

    outs = [half_shape, half_shape] + [quarter_shape] * 4
    mine, theirs, *quarters = call(
        rank_body, (), [SMEM, whole(layer_input)], [whole(a) for a in outs], outs
    )(sel, layer_input)
    theirs = swapped(theirs, "c")
    group = [quarters[0]]
    for k in (1, 2, 3):
        group.append(lax.ppermute(quarters[k], SEQ, [(i, i ^ k) for i in range(4)]))

    first = jnp.concatenate(slots[: nz // 4], axis=0)
    second = jnp.concatenate(slots[nz // 4 :], axis=0)
    first, second = lax.optimization_barrier((first, second, mine))[:2]

    def own_heads(array):
        own = lax.dynamic_slice_in_dim(array, core * wide, wide, axis=1)
        return own, lax.dynamic_slice_in_dim(array, (1 - core) * wide, wide, axis=1)

    x_own, x_sent = own_heads(head_input)
    goal_own, goal_sent = own_heads(targets)
    first = with_yh(first)
    second = with_x(second, nx)
    first, second = lax.optimization_barrier((first, second, x_sent, goal_sent))[:2]
    x_other, goal_other = swapped(x_sent, "c"), swapped(goal_sent, "c")
    part_a = with_x(first, nx)
    part_b = with_yh(second)

    def ordered(own, other):
        return jnp.where(core == 0, own, other), jnp.where(core == 0, other, own)

    xlo, xhi = ordered(x_own, x_other)
    glo, ghi = ordered(goal_own, goal_other)
    in_lo, in_hi = ordered(mine, theirs)
    chip_input = jnp.concatenate([in_lo, in_hi], axis=0)
    group_input = jnp.concatenate(group, axis=0)

    positions = yl * chip + jnp.arange(chip, dtype=jnp.int32)
    mask = jnp.any(positions[:, None] == mask_index[0][None, :], axis=1).astype(F32)[:, None]

    def by_core(table):
        own = lax.dynamic_slice_in_dim(table, core * 32, 32, axis=1).reshape(1, 64)
        return jnp.concatenate([own, own], axis=1)

    bias4, rate4 = by_core(dt_bias), by_core(rates)
    part_a, part_b, chip_input, xlo, xhi, glo, ghi, group_input, mask, bias4, rate4 = lax.optimization_barrier(
        (part_a, part_b, chip_input, xlo, xhi, glo, ghi, group_input, mask, bias4, rate4)
    )

    span = depth // 4
    projected = jnp.dot(chip_input[:, :span], part_a, preferred_element_type=F32) + jnp.dot(
        chip_input[:, span:], part_b, preferred_element_type=F32
    )
    projected_other = swapped(projected, "c")

    lanes = 64 * GROUP
    steps = wide // lanes
    outs = [
        shaped((chip, 512), BF16),
        shaped((chip, 384), BF16),
        shaped((steps, chip, 128), F32),
        shaped((128, chip), F32),
        shaped((chip, 128), F32),
        shaped((chip, 128), F32),
        shaped((128, wide), BF16),
    ]
    ins = [projected, projected_other, xlo, xhi, bias4, rate4]
    bc, ksp, kj, kt, fac, z4, leaving = call(
        prepare_kernel, (), [SMEM] + [whole(a) for a in ins], [whole(a) for a in outs], outs
    )(sel, *ins)
    entering = swapped(leaving, "yl")

    kt4 = kt[:64].reshape(2, steps, GROUP, chip)
    kt_spec = pl.BlockSpec((2, 1, GROUP, chip), lambda i: (0, i, 0, 0))
    kj_spec = pl.BlockSpec((1, chip, 128), lambda i: (i, 0, 0))
    big = lanes_block(chip, lanes)
    small = lanes_block(tokens, lanes)
    state_spec = lanes_block(128, lanes)
    wide_shape = shaped((chip, wide), BF16)
    square = pltpu.VMEM((2, chip, chip), F32)
    tables = pltpu.VMEM((2, 256, lanes), BF16)
    y_sd, y_rd = call(
        within_kernel,
        (steps,),
        [SMEM, kj_spec, kt_spec, whole(bc), small, small],
        [big] * 2,
        [wide_shape] * 2,
        [square, tables],
    )(sel, kj, kt4, bc, xlo, xhi)

    stats_shape = shaped((chip, 128), F32)
    y, stats = call(
        cross_kernel,
        (steps,),
        [SMEM, whole(bc), whole(fac), state_spec, big, big, small, small],
        [big, whole(stats_shape)],
        [wide_shape, stats_shape],
        [pltpu.VMEM((3, chip, 128), F32)],
    )(sel, bc, fac, entering, y_sd, y_rd, glo, ghi)
    stats_other = swapped(stats, "c")

    def loss_body(*refs):
        loss_kernel(*refs, count=features)

    go, direct = call(
        loss_body,
        (steps,),
        [SMEM, whole(stats), whole(stats), whole(mask), whole(bc), whole(fac), big, small, small],
        [big, state_spec],
        [wide_shape, shaped((128, wide), BF16)],
    )(sel, stats, stats_other, mask, bc, fac, y, glo, ghi)
    adjoint = swapped(direct, "yl")

    gbc_shape = shaped((chip, 512), F32)
    gxw, sums, gbc = call(
        back_within_kernel,
        (steps,),
        [SMEM, kj_spec, kt_spec, whole(bc), small, small, big, big, big],
        [big, whole(stats_shape), whole(gbc_shape)],
        [wide_shape, stats_shape, gbc_shape],
        [square, tables, square, pltpu.VMEM((chip, 128), F32), pltpu.VMEM((4 * lanes, 128), BF16)],
    )(sel, kj, kt4, bc, xlo, xhi, go, y, y_sd)

    grad_shape = shaped((chip, columns), F32)
    gx, grad = call(
        back_cross_kernel,
        (steps,),
        [SMEM, state_spec, state_spec]
        + [whole(a) for a in (bc, fac, ksp, z4, rate4)]
        + [small, small, big, big, whole(sums), whole(gbc)],
        [big, whole(grad_shape)],
        [wide_shape, grad_shape],
        [pltpu.VMEM((chip, 128), F32), pltpu.VMEM((2, chip, 128), F32)],
    )(sel, adjoint, entering, bc, fac, ksp, z4, rate4, xlo, xhi, go, gxw, sums, gbc)

    def by_owner(low, high):
        return jnp.where(core == 0, low, high), jnp.where(core == 0, high, low)

    grad_proj = (grad + swapped(grad, "c")).astype(BF16)
    grad_proj = jnp.concatenate(by_owner(grad_proj[:tokens], grad_proj[tokens:]), axis=0)
    grad_group = jnp.concatenate([grad_proj, swapped(grad_proj, "yl")], axis=0)
    grad_rows = lax.dot_general(
        group_input, grad_group, (((0,), (0,)), ((), ())), preferred_element_type=F32
    ).astype(BF16)
    grad_rows = grad_rows.reshape(2, nz // 2, nx, nyh, quarter, columns)
    sent = grad_rows[1, :, :, 1]
    second = grad_rows[1, :, :, 0].astype(F32) + swapped(sent, "yh").astype(F32)
    first = sum_over_x(grad_rows[0], nx).astype(BF16)
    second = sum_over_x(second.astype(BF16), nx)
    first = first[:, 0].astype(F32) + swapped(first[:, 1], "yh").astype(F32)
    total = jnp.concatenate([first, second], axis=0).astype(BF16)
    total = lax.all_to_all(total, "z", 0, 0, tiled=True)
    total = jnp.sum(total.astype(F32), axis=0)
    grad_weight = lax.all_gather(total, SEQ, axis=0, tiled=True)

    gx_own, gx_sent = by_owner(gx[:tokens], gx[tokens:])
    gx_other = swapped(gx_sent, "c")
    grad_x = jnp.concatenate(by_owner(gx_own, gx_other), axis=1)

    wide_grad = jnp.concatenate(
        [
            lax.dot_general(grad_proj, part, (((1,), (1,)), ((), ())), preferred_element_type=F32).astype(BF16)
            for part in (part_a, part_b)
        ],
        axis=1,
    )

    def unrank_body(*refs):
        unrank_kernel(*refs, sizes=sizes)

    grad_input = call(
        unrank_body,
        (),
        [SMEM, whole(half_shape), whole(half_shape)],
        whole(layer_input),
        shaped(layer_input.shape, BF16),
    )(sel, wide_grad[:tokens], swapped(wide_grad[tokens:], "c"))
    return grad_x, grad_input, grad_weight


def solution(mesh):
    sizes = fsdp_axes(mesh.shape["fsdp"])
    fine = Mesh(np.asarray(mesh.devices).reshape(*sizes, 2, 2), ("z", "x", "yh", "yl", "c"))
    fsdp = ("z", "x", "yh")
    tokens = P(fsdp + SEQ, None)
    rows = P(fsdp, None)

    def body(*arrays):
        return shards(sizes, *arrays)

    return jax.shard_map(
        body,
        mesh=fine,
        in_specs=(tokens, tokens, tokens, rows, P(), P(), rows),
        out_specs=(tokens, tokens, rows),
        check_vma=False,
    )
```

```python
import jax
import jax.numpy as jnp
import numpy as np
from jax import lax
from jax.experimental import pallas as pl
from jax.experimental.pallas import tpu as pltpu
from jax.sharding import Mesh
from jax.sharding import PartitionSpec as P

EPSILON = 1e-06
LOG2E = 1.4426950408889634
F32 = jnp.float32
BF16 = jnp.bfloat16
SEQ = ("yl", "c")
VMEM_LIMIT = 14 * 1024 * 1024
GROUP = 8


def fsdp_axes(count):
    return (count // 8, 4, 2)


def iota(shape, dim):
    return lax.broadcasted_iota(jnp.int32, shape, dim)


def mm(left, right):
    return lax.dot_general(left, right, (((1,), (0,)), ((), ())), preferred_element_type=F32)


def mm_nt(left, right):
    return lax.dot_general(left, right, (((1,), (1,)), ((), ())), preferred_element_type=F32)


def parts(value, count):
    pieces = []
    for _ in range(count):
        piece = value.astype(BF16)
        pieces.append(piece)
        value = value - piece.astype(F32)
    return jnp.concatenate(pieces, axis=1)


def as_bf16(condition):
    return jnp.where(condition, 1.0, 0.0).astype(BF16)


def exact_sum(mask, value):
    width = value.shape[1]
    out = mm(mask, parts(value, 3))
    return out[:, :width] + out[:, width : 2 * width] + out[:, 2 * width :]


def pick(value, chosen, pieces):
    rows, width = value.shape
    table = as_bf16(chosen(iota((pieces * width, width), 0) & (width - 1), iota((pieces * width, width), 1)))
    return mm(parts(value, pieces), table)


def spread_table(pieces, lane_base, lanes):
    shape = (pieces * 128, lanes)
    return as_bf16((iota(shape, 0) & 127) == lane_base + (iota(shape, 1) >> 6))


def block_at(z, core, i, count):
    half = count // 2
    return (jnp.where(core == 0, z + count - (half - 1 - i), z + i + 1)) & (count - 1)


def rank_kernel(sel, rows_in, mine, theirs, *quarters, sizes):
    nz, nx, nyh = sizes
    core, member, z, x, yh = sel[0], sel[2], sel[3], sel[4], sel[5]
    tokens = rows_in.shape[0]
    block = 128 * nx
    low_lanes = iota((tokens, 128), 1) < 64
    for out, owner in ((mine, core), (theirs, 1 - core)):
        for part in range(2):
            starts = [block_at(z, owner, 2 * part + i, nz) * block for i in range(2)]
            for xr in range(nx):
                at = ((x + nx - xr) & (nx - 1)) * 128
                tiles = [rows_in[:, pl.ds(pl.multiple_of(start + at, 128), 128)].astype(F32) for start in starts]
                low = jnp.where(low_lanes, tiles[0], pltpu.roll(tiles[1], 64, 1))
                high = jnp.where(low_lanes, pltpu.roll(tiles[0], 64, 1), tiles[1])
                for yr in range(nyh):
                    place = (xr * nyh + yr) if part == 0 else (yr * nx + xr)
                    to = part * 2 * block + place * 128
                    out[:, to : to + 128] = jnp.where(yh == yr, low, high).astype(BF16)
    dst = iota((1, block), 1)
    xr, yr = (dst >> 5) & (nx - 1), (dst >> 4) & 1
    source = ((x + xr) & (nx - 1)) * 128 + (yh ^ yr) * 64 + (member ^ (dst >> 7)) * 16 + (dst & 15)
    table = as_bf16(iota((block, block), 0) == source)
    for zz in range(nz):
        value = mm(rows_in[:, zz * block : (zz + 1) * block], table).astype(BF16)
        for k, out in enumerate(quarters):
            out[:, zz * 128 : (zz + 1) * 128] = value[:, k * 128 : (k + 1) * 128]


def unrank_kernel(sel, mine, theirs, out, *, sizes):
    nz, nx, nyh = sizes
    core, z, x, yh = sel[0], sel[3], sel[4], sel[5]
    tokens = out.shape[0]
    block = 128 * nx
    low_lanes = iota((tokens, 128), 1) < 64
    for ref, owner in ((mine, core), (theirs, 1 - core)):
        for part in range(2):
            starts = [block_at(z, owner, 2 * part + i, nz) * block for i in range(2)]
            for xr in range(nx):
                at = ((x + nx - xr) & (nx - 1)) * 128
                pair = []
                for yr in range(nyh):
                    place = (xr * nyh + yr) if part == 0 else (yr * nx + xr)
                    to = part * 2 * block + place * 128
                    pair.append(ref[:, to : to + 128].astype(F32))
                low = jnp.where(yh == 0, pair[0], pair[1])
                high = jnp.where(yh == 0, pair[1], pair[0])
                first = jnp.where(low_lanes, low, pltpu.roll(high, 64, 1))
                second = jnp.where(low_lanes, pltpu.roll(low, 64, 1), high)
                for start, tile in zip(starts, (first, second)):
                    out[:, pl.ds(pl.multiple_of(start + at, 128), 128)] = tile.astype(BF16)


def prepare_kernel(sel, pa, pb, xlo, xhi, bias, rate, bc_out, ksp_out, ks_out, kt_out, fac_out, z_out, state_out):
    tokens = pa.shape[0]
    core, sd = sel[0], sel[1]
    proj = pa[...] + pb[...]
    bc = proj[:, :512].astype(BF16)
    bc_out[...] = bc

    def source(row, col):
        return row == ((col >> 5) & 1) * 64 + core * 32 + (col & 31)

    z = pick(proj[:, 512:640], source, 3) + bias[...]
    z_out[...] = z
    step = jnp.maximum(z, 0.0) + jnp.log1p(jnp.exp(-jnp.abs(z)))
    g = -rate[...] * step * LOG2E
    row = iota((tokens, tokens), 0)
    col = iota((tokens, tokens), 1)
    low = exact_sum(as_bf16(col <= row), g)
    high = exact_sum(as_bf16(col >= row), g)
    lane = iota((tokens, 128), 1)
    first = ((lane >> 5) & 1) == 0
    k = jnp.where(first, low, high)
    total = jnp.where(first[:1], low[tokens - 1 :], high[:1])
    ks = jnp.where(lane < 64, k, step)
    ksp_out[...] = parts(ks, 3)
    kt_out[...] = ks.T
    ks_out[...] = ks
    leaving = jnp.exp2(total - k)
    fac_out[...] = jnp.where(lane < 64, jnp.exp2(k), leaving)
    factor = parts(step * leaving, 2)
    b_t = jnp.where(sd == 0, proj[:, :128], proj[:, 256:384]).T.astype(BF16)
    width = xlo.shape[1]
    for at in range(0, width, 256):
        table = spread_table(2, sd * 32 + at // 64, 256)
        x = jnp.concatenate([xlo[:, at : at + 256], xhi[:, at : at + 256]], axis=0)
        ve = (x.astype(F32) * mm(factor, table)).astype(BF16)
        state_out[:, at : at + 256] = mm(b_t, ve).astype(BF16)


def halves(value):
    first = (iota(value.shape, 1) & 64) == 0
    zero = jnp.zeros_like(value)
    return jnp.where(first, value, zero), jnp.where(first, zero, value)


def set_up(gram, tables, bc, lanes, transposed):
    half = bc.shape[0] // 2
    shape = (2 * half, 2 * half)
    row, col = iota(shape, 0), iota(shape, 1)
    for course in range(2):
        b_rows = bc[:, 256 * course : 256 * course + 128]
        c_rows = bc[:, 256 * course + 128 : 256 * course + 256]
        value = mm_nt(b_rows, c_rows) if transposed else mm_nt(c_rows, b_rows)
        keep = col <= row if (course == 0) != transposed else col >= row
        gram[course] = jnp.where(keep, value, 0.0)
        tables[course] = spread_table(2, 64 + 32 * course, lanes)


def within_kernel(sel, ks_ref, kt, fac, bc, xlo, xhi, y_sd, y_rd, entering, gram, tables):
    half = bc.shape[0] // 2
    sd = sel[1]

    @pl.when(pl.program_id(0) == 0)
    def _():
        set_up(gram, tables, bc, xlo.shape[1], False)

    x = jnp.concatenate([xlo[...], xhi[...]], axis=0).astype(F32)
    ks = pltpu.roll(ks_ref[...], 128 - GROUP * pl.program_id(0), 1)
    ks_parts = parts(ks, 2)
    results = []
    for course in range(2):
        v_a, v_b = halves((x * mm(ks_parts, tables[course])).astype(BF16))
        by_rows = []
        for tb in range(2):
            t_at = slice(tb * half, (tb + 1) * half)
            sources = range(tb + 1) if course == 0 else range(tb, 2)
            weights = [[] for _ in range(GROUP // 2)]
            values = [[] for _ in range(GROUP // 2)]
            for sb in sources:
                s_at = slice(sb * half, (sb + 1) * half)
                table = gram[course, t_at, s_at]
                for head in range(GROUP):
                    lane = 32 * course + head
                    gap = ks[t_at, lane : lane + 1] - kt[course, 0, head : head + 1, s_at]
                    if tb == sb:
                        gap = jnp.minimum(gap, 0.0)
                    pair = head // 2
                    weights[pair].append((jnp.exp2(gap) * table).astype(BF16))
                    values[pair].append((v_a, v_b)[head % 2][s_at, 128 * pair : 128 * pair + 128])
            by_rows.append(
                jnp.concatenate(
                    [
                        mm(jnp.concatenate(w, axis=1), jnp.concatenate(v, axis=0))
                        for w, v in zip(weights, values)
                    ],
                    axis=1,
                )
            )
        results.append(jnp.concatenate(by_rows, axis=0))
    y_sd[...] = jnp.where(sd == 0, results[0], results[1]).astype(BF16)
    y_rd[...] = jnp.where(sd == 0, results[1], results[0]).astype(BF16)
    factors = parts(fac[...], 2)
    lanes = xlo.shape[1]
    base = GROUP * pl.program_id(0)
    entering[...] = mm(factors, spread_table(2, (1 - sd) * 32 + base, lanes)).astype(BF16)


def cross_kernel(sel, bc, entering, state, y_sd, y_rd, glo, ghi, y_out, stats, acc):
    step = pl.program_id(0)
    lanes = state.shape[1]
    rd = 1 - sel[1]
    c_rows = jnp.where(rd == 0, bc[:, 128:256], bc[:, 384:512])
    carried = entering[...].astype(F32) * mm(c_rows, state[...])
    y = y_sd[...].astype(F32) + y_rd[...].astype(F32) + carried
    y_out[...] = y.astype(BF16)
    t = jnp.concatenate([glo[...], ghi[...]], axis=0).astype(F32)

    @pl.when(step == 0)
    def _():
        acc[...] = jnp.zeros_like(acc)

    for slot, value in enumerate((y * y, y * t, t * t)):
        total = value[:, :128]
        for at in range(128, lanes, 128):
            total = total + value[:, at : at + 128]
        acc[slot] += total

    @pl.when(step == pl.num_programs(0) - 1)
    def _():
        lane = iota(stats.shape, 1)
        out = jnp.zeros(stats.shape, F32)
        for slot in range(3):
            out = jnp.where(lane == slot, jnp.sum(acc[slot], axis=1, keepdims=True), out)
        stats[...] = out


def loss_kernel(
    sel, own, other, index, bc, entering, y_ref, y_sd, glo, ghi, go_out, direct_out, sums_out,
    y_scale, t_scale, place, *, count
):
    step = pl.program_id(0)
    lanes = glo.shape[1]
    rd = 1 - sel[1]

    @pl.when(step == 0)
    def _():
        stats = (own[...] + other[...]) * (1.0 / count)
        ry = jnp.sqrt(stats[:, 0:1] + EPSILON)
        rt = jnp.sqrt(stats[:, 2:3] + EPSILON)
        cosine = stats[:, 1:2] / (ry * rt)
        position = sel[1] * bc.shape[0] + iota((bc.shape[0], index.shape[1]), 0)
        masked = jnp.max(jnp.where(position == index[...], 1.0, 0.0), axis=1, keepdims=True) > 0.0
        y_scale[...] = jnp.broadcast_to(jnp.where(masked, cosine / (ry * ry), 0.0), y_scale.shape)
        place[...] = place_table(lanes, 64)
        sums_out[...] = jnp.zeros_like(sums_out)
        t_scale[...] = jnp.broadcast_to(jnp.where(masked, 1.0 / (rt * ry), 0.0), t_scale.shape)

    wide = (1, lanes // 128)
    t = jnp.concatenate([glo[...], ghi[...]], axis=0).astype(F32)
    y = y_ref[...].astype(F32)
    go = (jnp.tile(y_scale[...], wide) * y - jnp.tile(t_scale[...], wide) * t).astype(BF16)
    go_out[...] = go
    go_f = go.astype(F32)
    first = y_sd[...].astype(F32)
    rest = y - first
    products = [go_f * jnp.where(rd == 1, first, rest), go_f * jnp.where(rd == 1, rest, first)]
    gained = mm(jnp.concatenate([product.astype(BF16) for product in products], axis=1), place[...])
    sums_out[...] += pltpu.roll(gained, step * (lanes // 64), 1)
    scaled = (entering[...].astype(F32) * go_f).astype(BF16)
    c_t = jnp.where(rd == 0, bc[:, 128:256], bc[:, 384:512]).astype(F32).T.astype(BF16)
    direct_out[...] = mm(c_t, scaled).astype(BF16)


def place_table(lanes, base):
    shape = (2 * lanes, 128)
    row = iota(shape, 0)
    return as_bf16(iota(shape, 1) == base + (row // lanes) * 32 + ((row & (lanes - 1)) >> 6))


def back_within_kernel(
    sel, ks_ref, kt, fac, bc, xlo, xhi, go_ref, gx_out, sums_out, gbc_out, entering, leaving, sized,
    gram, tables, grad_gram, sums, place
):
    half = bc.shape[0] // 2
    step_at = pl.program_id(0)
    lanes = xlo.shape[1]
    sd = sel[1]

    @pl.when(step_at == 0)
    def _():
        set_up(gram, tables, bc, lanes, True)
        place[...] = place_table(lanes, 0)
        grad_gram[...] = jnp.zeros_like(grad_gram)
        sums[...] = jnp.zeros_like(sums)

    x = jnp.concatenate([xlo[...], xhi[...]], axis=0).astype(F32)
    go = go_ref[...]
    go_heads = halves(go)
    ks = pltpu.roll(ks_ref[...], 128 - GROUP * pl.program_id(0), 1)
    ks_parts = parts(ks, 2)
    grad_x = None
    products = []
    for course in range(2):
        step = mm(ks_parts, tables[course])
        v_heads = halves((x * step).astype(BF16))
        by_rows = []
        for sb in range(2):
            s_at = slice(sb * half, (sb + 1) * half)
            weights = [[] for _ in range(GROUP // 2)]
            values = [[] for _ in range(GROUP // 2)]
            for tb in (range(sb, 2) if course == 0 else range(sb + 1)):
                t_at = slice(tb * half, (tb + 1) * half)
                table = gram[course, s_at, t_at]
                gained = None
                for head in range(GROUP):
                    pair = head // 2
                    pair_at = slice(128 * pair, 128 * pair + 128)
                    lane = 32 * course + head
                    gap = kt[course, 0, head : head + 1, t_at] - ks[s_at, lane : lane + 1]
                    if tb == sb:
                        gap = jnp.minimum(gap, 0.0)
                    decay = jnp.exp2(gap)
                    weights[pair].append((decay * table).astype(BF16))
                    values[pair].append(go_heads[head % 2][t_at, pair_at])
                    term = mm_nt(v_heads[head % 2][s_at, pair_at], go[t_at, pair_at]) * decay
                    gained = term if gained is None else gained + term
                grad_gram[course, s_at, t_at] += gained
            by_rows.append(
                jnp.concatenate(
                    [
                        mm(jnp.concatenate(w, axis=1), jnp.concatenate(v, axis=0))
                        for w, v in zip(weights, values)
                    ],
                    axis=1,
                )
            )
        grad_v = jnp.concatenate(by_rows, axis=0)
        part = step * grad_v
        grad_x = part if grad_x is None else grad_x + part
        products.append((x * grad_v).astype(BF16))
    gx_out[...] = grad_x.astype(BF16)
    gained = mm(jnp.concatenate(products, axis=1), place[...])
    sums[...] += pltpu.roll(gained, GROUP * step_at, 1)
    factors = parts(fac[...], 2)
    entering[...] = mm(factors, spread_table(2, (1 - sd) * 32 + GROUP * step_at, lanes)).astype(BF16)
    left = mm(factors, spread_table(2, 64 + sd * 32 + GROUP * step_at, lanes))
    leaving[...] = left.astype(BF16)
    sized[...] = (left * mm(ks_parts, jnp.where(sd == 0, tables[0], tables[1]))).astype(BF16)

    @pl.when(step_at == pl.num_programs(0) - 1)
    def _():
        sums_out[...] = sums[...]
        shape = (2 * half, 2 * half)
        row, col = iota(shape, 0), iota(shape, 1)
        for course in range(2):
            keep = row <= col if course == 0 else row >= col
            gg = jnp.where(keep, grad_gram[course], 0.0)
            at = 256 * course
            gbc_out[:, at : at + 128] = mm(gg.astype(BF16), bc[:, at + 128 : at + 256])
            gbc_out[:, at + 128 : at + 256] = mm(gg.T.astype(BF16), bc[:, at : at + 128])


def back_cross_kernel(
    sel, adjoint, state, bc, ksp, z_ref, rate, entering, leaving, sized, xlo, xhi, go_ref, gxw, sums_in, gy, gbc_in, gx_own, gx_sent, grad_out, sums, grads
):
    step = pl.program_id(0)
    lanes = xlo.shape[1]
    tokens = bc.shape[0]
    core, sd = sel[0], sel[1]
    rd = 1 - sd
    heads = lanes // 64

    @pl.when(step == 0)
    def _():
        sums[...] = jnp.zeros_like(sums)
        grads[...] = jnp.zeros_like(grads)

    x = jnp.concatenate([xlo[...], xhi[...]], axis=0).astype(F32)
    b_rows = jnp.where(sd == 0, bc[:, :128], bc[:, 256:384])
    met = mm(b_rows, adjoint[...])
    size = sized[...].astype(F32)
    grad_x = (gxw[...].astype(F32) + size * met).astype(BF16)
    low, high = grad_x[: tokens // 2], grad_x[tokens // 2 :]
    gx_own[...] = jnp.where(core == 0, low, high)
    gx_sent[...] = jnp.where(core == 0, high, low)
    product = x * met * leaving[...].astype(F32)
    shape = (lanes, 128)
    row, col = iota(shape, 0), iota(shape, 1)
    target = sd * 32 + step * heads + ((row & (lanes - 1)) >> 6)
    sums[...] += mm(product.astype(BF16), as_bf16(col == target))
    ve = (x * size).astype(BF16)
    grads[0] += mm_nt(ve, adjoint[...])
    scaled = (entering[...].astype(F32) * go_ref[...].astype(F32)).astype(BF16)
    grads[1] += mm_nt(scaled, state[...])

    @pl.when(step == pl.num_programs(0) - 1)
    def _():
        within = sums_in[...] + gy[...]
        cross = sums[...]
        size4 = ksp[:, :128].astype(F32) + ksp[:, 128:256].astype(F32) + ksp[:, 256:].astype(F32)
        lane = iota((tokens, 128), 1)
        size4 = jnp.where(lane < 64, pltpu.roll(size4, 64, 1), size4)
        moved = pltpu.roll(within, 64, 1)
        rs = within + cross
        grad_k = moved - size4 * rs
        r_total = jnp.sum(size4 * cross, axis=0, keepdims=True)
        trow, tcol = iota((tokens, tokens), 0), iota((tokens, tokens), 1)
        later = exact_sum(as_bf16(tcol >= trow), grad_k)
        earlier = exact_sum(as_bf16(tcol <= trow), grad_k)
        grad_g = jnp.where(lane < 32, later, earlier) + r_total
        sigma = 1.0 / (1.0 + jnp.exp(-z_ref[...]))
        grad_z = jnp.where(lane < 64, (rs - rate[...] * grad_g) * sigma, 0.0)

        def place(row_at, col_at):
            return (row_at < 64) & (col_at == ((row_at >> 5) & 1) * 64 + core * 32 + (row_at & 31))

        grad_out[:, 512:640] = pick(grad_z, place, 3)
        gbc = gbc_in[...]
        grad_out[:, 0:128] = gbc[:, 0:128] + jnp.where(sd == 0, grads[0], 0.0)
        grad_out[:, 128:256] = gbc[:, 128:256] + jnp.where(rd == 0, grads[1], 0.0)
        grad_out[:, 256:384] = gbc[:, 256:384] + jnp.where(sd == 1, grads[0], 0.0)
        grad_out[:, 384:512] = gbc[:, 384:512] + jnp.where(rd == 1, grads[1], 0.0)


def shaped(shape, dtype):
    return jax.ShapeDtypeStruct(shape, dtype)


SMEM = pl.BlockSpec(memory_space=pltpu.SMEM)


def whole(array):
    rank = len(array.shape)
    return pl.BlockSpec(array.shape, lambda *_: (0,) * rank)


def lanes_block(rows, lanes):
    return pl.BlockSpec((rows, lanes), lambda i: (0, i))


def call(body, mega_flops, grid, in_specs, out_specs, out_shape, scratch=()):
    return pl.pallas_call(
        body,
        grid=grid,
        in_specs=in_specs,
        out_specs=out_specs,
        out_shape=out_shape,
        scratch_shapes=list(scratch),
        cost_estimate=pl.CostEstimate(flops=mega_flops * 1000000, bytes_accessed=0, transcendentals=0),
        compiler_params=pltpu.CompilerParams(vmem_limit_bytes=VMEM_LIMIT),
    )


def ring(count, distance):
    return [(i, (i + distance) % count) for i in range(count)]


def swapped(value, axis):
    return lax.ppermute(value, axis, [(0, 1), (1, 0)])


def gather_along_z(weight, count):
    half = count // 2
    slots = []
    for i in range(half):
        route = []
        for z in range(count):
            route.append((2 * z, 2 * ((z + half - 1 - i) % count)))
            route.append((2 * z + 1, 2 * ((z - i - 1) % count) + 1))
        slots.append(lax.ppermute(weight, ("z", "c"), route))
    return slots


def with_x(value, count):
    return jnp.concatenate([value] + [lax.ppermute(value, "x", ring(count, k)) for k in range(1, count)], axis=0)


def over_yh(value):
    return lax.ppermute(value, ("yh", "yl"), [(i, 3 - i) for i in range(4)])


def with_yh(value):
    return jnp.concatenate([value, over_yh(value)], axis=0)


def sum_over_x(value, count):
    total = value[:, 0].astype(F32)
    for k in range(1, count):
        total = total + lax.ppermute(value[:, k], "x", ring(count, k)).astype(F32)
    return total


def shards(sizes, layer_input, head_input, targets, proj_weight, rates, dt_bias, mask_index):
    nz, nx, nyh = sizes
    z, x, yh = (lax.axis_index(name) for name in ("z", "x", "yh"))
    yl, core = lax.axis_index("yl"), lax.axis_index("c")
    tokens, depth = layer_input.shape
    features = head_input.shape[1]
    wide = features // 2
    rows, columns = proj_weight.shape
    chip = 2 * tokens
    quarter = rows // 4
    sel = jnp.stack([core, yl, 2 * (yl ^ yh) + core, z, x, yh]).astype(jnp.int32)

    slots = gather_along_z(proj_weight, nz)

    half_shape = shaped((tokens, depth // 2), BF16)
    quarter_shape = shaped((tokens, depth // 4), BF16)

    def rank_body(*refs):
        rank_kernel(*refs, sizes=sizes)

    outs = [half_shape, half_shape] + [quarter_shape] * 4
    mine, theirs, *quarters = call(
        rank_body, 2640, (), [SMEM, whole(layer_input)], [whole(a) for a in outs], outs
    )(sel, layer_input)

    def own_heads(array):
        own = lax.dynamic_slice_in_dim(array, core * wide, wide, axis=1)
        return own, lax.dynamic_slice_in_dim(array, (1 - core) * wide, wide, axis=1)

    def ordered(own, other):
        return jnp.where(core == 0, own, other), jnp.where(core == 0, other, own)

    def by_core(table):
        own = lax.dynamic_slice_in_dim(table, core * 32, 32, axis=1).reshape(1, 64)
        return jnp.concatenate([own, own], axis=1)

    x_own, x_sent = own_heads(head_input)
    goal_own, goal_sent = own_heads(targets)
    x_other = swapped(x_sent, "c")
    first = jnp.concatenate(slots[: nz // 4], axis=0)
    second = jnp.concatenate(slots[nz // 4 :], axis=0)
    first, second, theirs, x_other = lax.optimization_barrier((first, second, theirs, x_other))
    theirs = swapped(theirs, "c")
    first = with_yh(first)
    second = with_x(second, nx)
    first, second, theirs, quarters[2], quarters[3] = lax.optimization_barrier(
        (first, second, theirs, quarters[2], quarters[3])
    )
    group = {0: quarters[0]}
    for k in (2, 3):
        group[k] = lax.ppermute(quarters[k], SEQ, [(i, i ^ k) for i in range(4)])
    part_a = with_x(first, nx)
    part_b = with_yh(second)
    xlo, xhi = ordered(x_own, x_other)
    chip_input = jnp.concatenate(ordered(mine, theirs), axis=0)
    bias4, rate4 = by_core(dt_bias), by_core(rates)
    part_a, part_b, chip_input, xlo, xhi, bias4, rate4, goal_sent, quarters[1], group[2], group[3] = (
        lax.optimization_barrier(
            (part_a, part_b, chip_input, xlo, xhi, bias4, rate4, goal_sent, quarters[1], group[2], group[3])
        )
    )
    group[1] = swapped(quarters[1], "c")

    span = depth // 4
    projected = jnp.dot(chip_input[:, :span], part_a, preferred_element_type=F32) + jnp.dot(
        chip_input[:, span:], part_b, preferred_element_type=F32
    )
    projected_other = swapped(projected, "c")

    lanes = 64 * GROUP
    steps = wide // lanes
    outs = [
        shaped((chip, 512), BF16),
        shaped((chip, 384), BF16),
        shaped((chip, 128), F32),
        shaped((128, chip), F32),
        shaped((chip, 128), F32),
        shaped((chip, 128), F32),
        shaped((128, wide), BF16),
    ]
    ins = [projected, projected_other, xlo, xhi, bias4, rate4]
    bc, ksp, ks, kt, fac, z4, leaving = call(
        prepare_kernel, 3190, (), [SMEM] + [whole(a) for a in ins], [whole(a) for a in outs], outs
    )(sel, *ins)
    goal_sent, bc = lax.optimization_barrier((goal_sent, bc))
    glo, ghi = ordered(goal_own, swapped(goal_sent, "c"))
    state = swapped(leaving, "yl")

    kt4 = kt[:64].reshape(2, steps, GROUP, chip)
    kt_spec = pl.BlockSpec((2, 1, GROUP, chip), lambda i: (0, i, 0, 0))
    big = lanes_block(chip, lanes)
    small = lanes_block(tokens, lanes)
    state_spec = lanes_block(128, lanes)
    wide_shape = shaped((chip, wide), BF16)
    wide_half = shaped((tokens, wide), BF16)
    square = pltpu.VMEM((2, chip, chip), F32)
    tables = pltpu.VMEM((2, 256, lanes), BF16)
    y_sd, y_rd, entering = call(
        within_kernel, 6160,
        (steps,),
        [SMEM, whole(ks), kt_spec, whole(fac), whole(bc), small, small],
        [big] * 3,
        [wide_shape] * 3,
        [square, tables],
    )(sel, ks, kt4, fac, bc, xlo, xhi)


    stats_shape = shaped((chip, 128), F32)
    y, stats = call(
        cross_kernel, 3080,
        (steps,),
        [SMEM, whole(bc), big, state_spec, big, big, small, small],
        [big, whole(stats_shape)],
        [wide_shape, stats_shape],
        [pltpu.VMEM((3, chip, 128), F32)],
    )(sel, bc, entering, state, y_sd, y_rd, glo, ghi)
    stats_other = swapped(stats, "c")

    def loss_body(*refs):
        loss_kernel(*refs, count=features)

    go, direct, gy = call(
        loss_body, 3300,
        (steps,),
        [SMEM, whole(stats), whole(stats), whole(mask_index), whole(bc), big, big, big, small, small],
        [big, state_spec, whole(stats_shape)],
        [wide_shape, shaped((128, wide), BF16), stats_shape],
        [pltpu.VMEM((chip, 128), F32), pltpu.VMEM((chip, 128), F32), pltpu.VMEM((2 * lanes, 128), BF16)],
    )(sel, stats, stats_other, mask_index, bc, entering, y, y_sd, glo, ghi)
    adjoint = swapped(direct, "yl")
    group_input = jnp.concatenate(ordered(group[0], group[1]) + ordered(group[2], group[3]), axis=0)

    gbc_shape = shaped((chip, 512), F32)
    gxw, sums, gbc, entering, leaving, sized = call(
        back_within_kernel, 12650,
        (steps,),
        [SMEM, whole(ks), kt_spec, whole(fac), whole(bc), small, small, big],
        [big, whole(stats_shape), whole(gbc_shape), big, big, big],
        [wide_shape, stats_shape, gbc_shape, wide_shape, wide_shape, wide_shape],
        [square, tables, square, pltpu.VMEM((chip, 128), F32), pltpu.VMEM((2 * lanes, 128), BF16)],
    )(sel, ks, kt4, fac, bc, xlo, xhi, go)

    grad_shape = shaped((chip, columns), F32)
    gx_own, gx_sent, grad = call(
        back_cross_kernel, 4950,
        (steps,),
        [SMEM, state_spec, state_spec]
        + [whole(a) for a in (bc, ksp, z4, rate4)]
        + [big, big, big, small, small, big, big, whole(sums), whole(gy), whole(gbc)],
        [small, small, whole(grad_shape)],
        [wide_half, wide_half, grad_shape],
        [pltpu.VMEM((chip, 128), F32), pltpu.VMEM((2, chip, 128), F32)],
    )(sel, adjoint, state, bc, ksp, z4, rate4, entering, leaving, sized, xlo, xhi, go, gxw, sums, gy, gbc)

    def by_owner(low, high):
        return jnp.where(core == 0, low, high), jnp.where(core == 0, high, low)

    grad_proj = (grad + swapped(grad, "c")).astype(BF16)
    grad_group = jnp.concatenate([grad_proj, swapped(grad_proj, "yl")], axis=0)

    def weight_rows(columns_at):
        value = lax.dot_general(
            columns_at, grad_group, (((0,), (0,)), ((), ())), preferred_element_type=F32
        ).astype(BF16)
        return value.reshape(-1, nx, nyh, quarter, columns)

    cut = (5 * nz // 8) * (depth // 4 // nz)
    second = weight_rows(group_input[:, cut:])
    second = second[:, :, 0].astype(F32) + over_yh(second[:, :, 1]).astype(F32)
    first = weight_rows(group_input[:, :cut])
    first = sum_over_x(first, nx).astype(BF16)
    second = sum_over_x(second.astype(BF16), nx)
    first = first[:, 0].astype(F32) + over_yh(first[:, 1]).astype(F32)
    total = jnp.concatenate([first, second], axis=0).astype(BF16)
    total = lax.all_to_all(total, "z", 0, 0, tiled=True)
    total = jnp.sum(total.astype(F32), axis=0)
    grad_weight = lax.all_gather(
        total, ("yh",) + SEQ, axis=0, tiled=True, axis_index_groups=[[0, 1, 2, 3], [6, 7, 4, 5]]
    )

    def owned_and_received(value):
        own, sent = by_owner(value[:tokens], value[tokens:])
        return own, swapped(sent, "c")

    grad_x = jnp.concatenate(by_owner(gx_own, swapped(gx_sent, "c")), axis=1)

    wide_grad = jnp.concatenate(
        [
            lax.dot_general(grad_proj, part, (((1,), (1,)), ((), ())), preferred_element_type=F32).astype(BF16)
            for part in (part_a, part_b)
        ],
        axis=1,
    )

    def unrank_body(*refs):
        unrank_kernel(*refs, sizes=sizes)

    grad_input = call(
        unrank_body, 2200,
        (),
        [SMEM, whole(half_shape), whole(half_shape)],
        whole(layer_input),
        shaped(layer_input.shape, BF16),
    )(sel, *owned_and_received(wide_grad))
    return grad_x, grad_input, grad_weight


def solution(mesh):
    sizes = fsdp_axes(mesh.shape["fsdp"])
    fine = Mesh(np.asarray(mesh.devices).reshape(*sizes, 2, 2), ("z", "x", "yh", "yl", "c"))
    fsdp = ("z", "x", "yh")
    tokens = P(fsdp + SEQ, None)
    rows = P(fsdp, None)

    def body(*arrays):
        return shards(sizes, *arrays)

    return jax.shard_map(
        body,
        mesh=fine,
        in_specs=(tokens, tokens, tokens, rows, P(), P(), rows),
        out_specs=(tokens, tokens, rows),
        check_vma=False,
    )
```

```python
import jax
import jax.numpy as jnp
import numpy as np
from jax import lax
from jax.experimental import pallas as pl
from jax.experimental.pallas import tpu as pltpu
from jax.sharding import Mesh
from jax.sharding import PartitionSpec as P

EPSILON = 1e-06
LOG2E = 1.4426950408889634
F32 = jnp.float32
BF16 = jnp.bfloat16
SEQ = ("yl", "c")
VMEM_LIMIT = 14 * 1024 * 1024
GROUP = 8


def fsdp_axes(count):
    return (count // 8, 4, 2)


def iota(shape, dim):
    return lax.broadcasted_iota(jnp.int32, shape, dim)


def mm(left, right):
    return lax.dot_general(left, right, (((1,), (0,)), ((), ())), preferred_element_type=F32)


def mm_nt(left, right):
    return lax.dot_general(left, right, (((1,), (1,)), ((), ())), preferred_element_type=F32)


def parts(value, count):
    pieces = []
    for _ in range(count):
        piece = value.astype(BF16)
        pieces.append(piece)
        value = value - piece.astype(F32)
    return jnp.concatenate(pieces, axis=1)


def as_bf16(condition):
    return jnp.where(condition, 1.0, 0.0).astype(BF16)


def exact_sum(mask, value):
    width = value.shape[1]
    out = mm(mask, parts(value, 3))
    return out[:, :width] + out[:, width : 2 * width] + out[:, 2 * width :]


def pick(value, chosen, pieces):
    rows, width = value.shape
    table = as_bf16(chosen(iota((pieces * width, width), 0) & (width - 1), iota((pieces * width, width), 1)))
    return mm(parts(value, pieces), table)


def spread_table(pieces, lane_base, lanes):
    shape = (pieces * 128, lanes)
    return as_bf16((iota(shape, 0) & 127) == lane_base + (iota(shape, 1) >> 6))


def block_at(z, core, i, count):
    half = count // 2
    return (jnp.where(core == 0, z + count - (half - 1 - i), z + i + 1)) & (count - 1)


def rank_kernel(sel, rows_in, mine, theirs, *quarters, sizes):
    nz, nx, nyh = sizes
    core, member, z, x, yh = sel[0], sel[2], sel[3], sel[4], sel[5]
    tokens = rows_in.shape[0]
    block = 128 * nx
    low_lanes = iota((tokens, 128), 1) < 64
    for out, owner in ((mine, core), (theirs, 1 - core)):
        for part in range(2):
            starts = [block_at(z, owner, 2 * part + i, nz) * block for i in range(2)]
            for xr in range(nx):
                at = ((x + nx - xr) & (nx - 1)) * 128
                tiles = [rows_in[:, pl.ds(pl.multiple_of(start + at, 128), 128)].astype(F32) for start in starts]
                low = jnp.where(low_lanes, tiles[0], pltpu.roll(tiles[1], 64, 1))
                high = jnp.where(low_lanes, pltpu.roll(tiles[0], 64, 1), tiles[1])
                for yr in range(nyh):
                    place = (xr * nyh + yr) if part == 0 else (yr * nx + xr)
                    to = part * 2 * block + place * 128
                    out[:, to : to + 128] = jnp.where(yh == yr, low, high).astype(BF16)
    dst = iota((1, block), 1)
    xr, yr = (dst >> 5) & (nx - 1), (dst >> 4) & 1
    source = ((x + xr) & (nx - 1)) * 128 + (yh ^ yr) * 64 + (member ^ (dst >> 7)) * 16 + (dst & 15)
    table = as_bf16(iota((block, block), 0) == source)
    for zz in range(nz):
        value = mm(rows_in[:, zz * block : (zz + 1) * block], table).astype(BF16)
        for k, out in enumerate(quarters):
            out[:, zz * 128 : (zz + 1) * 128] = value[:, k * 128 : (k + 1) * 128]


def unrank_kernel(sel, mine, theirs, out, *, sizes):
    nz, nx, nyh = sizes
    core, z, x, yh = sel[0], sel[3], sel[4], sel[5]
    tokens = out.shape[0]
    block = 128 * nx
    low_lanes = iota((tokens, 128), 1) < 64
    for ref, owner in ((mine, core), (theirs, 1 - core)):
        for part in range(2):
            starts = [block_at(z, owner, 2 * part + i, nz) * block for i in range(2)]
            for xr in range(nx):
                at = ((x + nx - xr) & (nx - 1)) * 128
                pair = []
                for yr in range(nyh):
                    place = (xr * nyh + yr) if part == 0 else (yr * nx + xr)
                    to = part * 2 * block + place * 128
                    pair.append(ref[:, to : to + 128].astype(F32))
                low = jnp.where(yh == 0, pair[0], pair[1])
                high = jnp.where(yh == 0, pair[1], pair[0])
                first = jnp.where(low_lanes, low, pltpu.roll(high, 64, 1))
                second = jnp.where(low_lanes, pltpu.roll(low, 64, 1), high)
                for start, tile in zip(starts, (first, second)):
                    out[:, pl.ds(pl.multiple_of(start + at, 128), 128)] = tile.astype(BF16)


def prepare_kernel(sel, pa, pb, xlo, xhi, bias, rate, bc_out, ksp_out, ks_out, kt_out, fac_out, z_out, state_out):
    tokens = pa.shape[0]
    core, sd = sel[0], sel[1]
    proj = pa[...] + pb[...]
    bc = proj[:, :512].astype(BF16)
    bc_out[...] = bc

    def source(row, col):
        return row == ((col >> 5) & 1) * 64 + core * 32 + (col & 31)

    z = pick(proj[:, 512:640], source, 3) + bias[...]
    z_out[...] = z
    step = jnp.maximum(z, 0.0) + jnp.log1p(jnp.exp(-jnp.abs(z)))
    g = -rate[...] * step * LOG2E
    row = iota((tokens, tokens), 0)
    col = iota((tokens, tokens), 1)
    low = exact_sum(as_bf16(col <= row), g)
    high = exact_sum(as_bf16(col >= row), g)
    lane = iota((tokens, 128), 1)
    first = ((lane >> 5) & 1) == 0
    k = jnp.where(first, low, high)
    total = jnp.where(first[:1], low[tokens - 1 :], high[:1])
    ks = jnp.where(lane < 64, k, step)
    ksp_out[...] = parts(ks, 3)
    kt_out[...] = ks.T
    ks_out[...] = ks
    leaving = jnp.exp2(total - k)
    fac_out[...] = jnp.where(lane < 64, jnp.exp2(k), leaving)
    factor = parts(step * leaving, 2)
    b_t = jnp.where(sd == 0, proj[:, :128], proj[:, 256:384]).T.astype(BF16)
    width = xlo.shape[1]
    for at in range(0, width, 256):
        table = spread_table(2, sd * 32 + at // 64, 256)
        x = jnp.concatenate([xlo[:, at : at + 256], xhi[:, at : at + 256]], axis=0)
        ve = (x.astype(F32) * mm(factor, table)).astype(BF16)
        state_out[:, at : at + 256] = mm(b_t, ve).astype(BF16)


def halves(value):
    first = (iota(value.shape, 1) & 64) == 0
    zero = jnp.zeros_like(value)
    return jnp.where(first, value, zero), jnp.where(first, zero, value)


def set_up(gram, tables, bc, lanes, transposed):
    half = bc.shape[0] // 2
    shape = (2 * half, 2 * half)
    row, col = iota(shape, 0), iota(shape, 1)
    for course in range(2):
        b_rows = bc[:, 256 * course : 256 * course + 128]
        c_rows = bc[:, 256 * course + 128 : 256 * course + 256]
        value = mm_nt(b_rows, c_rows) if transposed else mm_nt(c_rows, b_rows)
        keep = col <= row if (course == 0) != transposed else col >= row
        gram[course] = jnp.where(keep, value, 0.0)
        tables[course] = spread_table(2, 64 + 32 * course, lanes)


def within_kernel(sel, ks_ref, kt, fac, bc, xlo, xhi, y_sd, y_rd, entering, gram, tables):
    half = bc.shape[0] // 2
    sd = sel[1]

    @pl.when(pl.program_id(0) == 0)
    def _():
        set_up(gram, tables, bc, xlo.shape[1], False)

    x = jnp.concatenate([xlo[...], xhi[...]], axis=0).astype(F32)
    ks = pltpu.roll(ks_ref[...], 128 - GROUP * pl.program_id(0), 1)
    ks_parts = parts(ks, 2)
    results = []
    for course in range(2):
        v_a, v_b = halves((x * mm(ks_parts, tables[course])).astype(BF16))
        by_rows = []
        for tb in range(2):
            t_at = slice(tb * half, (tb + 1) * half)
            sources = range(tb + 1) if course == 0 else range(tb, 2)
            weights = [[] for _ in range(GROUP // 2)]
            values = [[] for _ in range(GROUP // 2)]
            for sb in sources:
                s_at = slice(sb * half, (sb + 1) * half)
                table = gram[course, t_at, s_at]
                for head in range(GROUP):
                    lane = 32 * course + head
                    gap = ks[t_at, lane : lane + 1] - kt[course, 0, head : head + 1, s_at]
                    if tb == sb:
                        gap = jnp.minimum(gap, 0.0)
                    pair = head // 2
                    weights[pair].append((jnp.exp2(gap) * table).astype(BF16))
                    values[pair].append((v_a, v_b)[head % 2][s_at, 128 * pair : 128 * pair + 128])
            by_rows.append(
                jnp.concatenate(
                    [
                        mm(jnp.concatenate(w, axis=1), jnp.concatenate(v, axis=0))
                        for w, v in zip(weights, values)
                    ],
                    axis=1,
                )
            )
        results.append(jnp.concatenate(by_rows, axis=0))
    y_sd[...] = jnp.where(sd == 0, results[0], results[1]).astype(BF16)
    y_rd[...] = jnp.where(sd == 0, results[1], results[0]).astype(BF16)
    factors = parts(fac[...], 2)
    lanes = xlo.shape[1]
    base = GROUP * pl.program_id(0)
    entering[...] = mm(factors, spread_table(2, (1 - sd) * 32 + base, lanes)).astype(BF16)


def cross_kernel(sel, bc, entering, state, y_sd, y_rd, glo, ghi, y_out, stats, acc):
    step = pl.program_id(0)
    lanes = state.shape[1]
    rd = 1 - sel[1]
    c_rows = jnp.where(rd == 0, bc[:, 128:256], bc[:, 384:512])
    carried = entering[...].astype(F32) * mm(c_rows, state[...])
    y = y_sd[...].astype(F32) + y_rd[...].astype(F32) + carried
    y_out[...] = y.astype(BF16)
    t = jnp.concatenate([glo[...], ghi[...]], axis=0).astype(F32)

    @pl.when(step == 0)
    def _():
        acc[...] = jnp.zeros_like(acc)

    for slot, value in enumerate((y * y, y * t, t * t)):
        total = value[:, :128]
        for at in range(128, lanes, 128):
            total = total + value[:, at : at + 128]
        acc[slot] += total

    @pl.when(step == pl.num_programs(0) - 1)
    def _():
        lane = iota(stats.shape, 1)
        out = jnp.zeros(stats.shape, F32)
        for slot in range(3):
            out = jnp.where(lane == slot, jnp.sum(acc[slot], axis=1, keepdims=True), out)
        stats[...] = out


def loss_kernel(sel, own, other, index, bc, entering, y_ref, glo, ghi, go_out, direct_out, y_scale, t_scale, *, count):
    step = pl.program_id(0)
    lanes = glo.shape[1]
    rd = 1 - sel[1]

    @pl.when(step == 0)
    def _():
        stats = (own[...] + other[...]) * (1.0 / count)
        ry = jnp.sqrt(stats[:, 0:1] + EPSILON)
        rt = jnp.sqrt(stats[:, 2:3] + EPSILON)
        cosine = stats[:, 1:2] / (ry * rt)
        position = sel[1] * bc.shape[0] + iota((bc.shape[0], index.shape[1]), 0)
        masked = jnp.max(jnp.where(position == index[...], 1.0, 0.0), axis=1, keepdims=True) > 0.0
        y_scale[...] = jnp.broadcast_to(jnp.where(masked, cosine / (ry * ry), 0.0), y_scale.shape)
        t_scale[...] = jnp.broadcast_to(jnp.where(masked, 1.0 / (rt * ry), 0.0), t_scale.shape)

    wide = (1, lanes // 128)
    t = jnp.concatenate([glo[...], ghi[...]], axis=0).astype(F32)
    y = y_ref[...].astype(F32)
    go = (jnp.tile(y_scale[...], wide) * y - jnp.tile(t_scale[...], wide) * t).astype(BF16)
    go_out[...] = go
    go_f = go.astype(F32)
    scaled = (entering[...].astype(F32) * go_f).astype(BF16)
    c_t = jnp.where(rd == 0, bc[:, 128:256], bc[:, 384:512]).astype(F32).T.astype(BF16)
    direct_out[...] = mm(c_t, scaled).astype(BF16)


def place_table(lanes):
    shape = (4 * lanes, 128)
    row = iota(shape, 0)
    return as_bf16(iota(shape, 1) == (row // lanes) * 32 + ((row & (lanes - 1)) >> 6))


def back_within_kernel(
    sel, ks_ref, kt, fac, bc, xlo, xhi, go_ref, y_ref, y_sd, entering, state,
    gx_out, sums_out, gbc_out, leaving, sized, gram, tables, grad_gram, sums, grad_c, place
):
    half = bc.shape[0] // 2
    step_at = pl.program_id(0)
    lanes = xlo.shape[1]
    sd = sel[1]

    @pl.when(step_at == 0)
    def _():
        set_up(gram, tables, bc, lanes, True)
        place[...] = place_table(lanes)
        grad_c[...] = jnp.zeros_like(grad_c)
        grad_gram[...] = jnp.zeros_like(grad_gram)
        sums[...] = jnp.zeros_like(sums)

    x = jnp.concatenate([xlo[...], xhi[...]], axis=0).astype(F32)
    go = go_ref[...]
    go_heads = halves(go)
    ks = pltpu.roll(ks_ref[...], 128 - GROUP * pl.program_id(0), 1)
    ks_parts = parts(ks, 2)
    grad_x = None
    products = []
    for course in range(2):
        step = mm(ks_parts, tables[course])
        v_heads = halves((x * step).astype(BF16))
        by_rows = []
        for sb in range(2):
            s_at = slice(sb * half, (sb + 1) * half)
            weights = [[] for _ in range(GROUP // 2)]
            values = [[] for _ in range(GROUP // 2)]
            for tb in (range(sb, 2) if course == 0 else range(sb + 1)):
                t_at = slice(tb * half, (tb + 1) * half)
                table = gram[course, s_at, t_at]
                gained = None
                for head in range(GROUP):
                    pair = head // 2
                    pair_at = slice(128 * pair, 128 * pair + 128)
                    lane = 32 * course + head
                    gap = kt[course, 0, head : head + 1, t_at] - ks[s_at, lane : lane + 1]
                    if tb == sb:
                        gap = jnp.minimum(gap, 0.0)
                    decay = jnp.exp2(gap)
                    weights[pair].append((decay * table).astype(BF16))
                    values[pair].append(go_heads[head % 2][t_at, pair_at])
                    term = mm_nt(v_heads[head % 2][s_at, pair_at], go[t_at, pair_at]) * decay
                    gained = term if gained is None else gained + term
                grad_gram[course, s_at, t_at] += gained
            by_rows.append(
                jnp.concatenate(
                    [
                        mm(jnp.concatenate(w, axis=1), jnp.concatenate(v, axis=0))
                        for w, v in zip(weights, values)
                    ],
                    axis=1,
                )
            )
        grad_v = jnp.concatenate(by_rows, axis=0)
        part = step * grad_v
        grad_x = part if grad_x is None else grad_x + part
        products.append((x * grad_v).astype(BF16))
    gx_out[...] = grad_x.astype(BF16)
    go_f = go.astype(F32)
    own = y_sd[...].astype(F32)
    rest = y_ref[...].astype(F32) - own
    products.append((go_f * jnp.where(sd == 0, own, rest)).astype(BF16))
    products.append((go_f * jnp.where(sd == 0, rest, own)).astype(BF16))
    scaled = (entering[...].astype(F32) * go_f).astype(BF16)
    grad_c[...] += mm_nt(scaled, state[...])
    gained = mm(jnp.concatenate(products, axis=1), place[...])
    sums[...] += pltpu.roll(gained, GROUP * step_at, 1)
    factors = parts(fac[...], 2)
    left = mm(factors, spread_table(2, 64 + sd * 32 + GROUP * step_at, lanes))
    leaving[...] = left.astype(BF16)
    sized[...] = (left * mm(ks_parts, jnp.where(sd == 0, tables[0], tables[1]))).astype(BF16)

    @pl.when(step_at == pl.num_programs(0) - 1)
    def _():
        sums_out[...] = sums[...]
        shape = (2 * half, 2 * half)
        row, col = iota(shape, 0), iota(shape, 1)
        for course in range(2):
            keep = row <= col if course == 0 else row >= col
            gg = jnp.where(keep, grad_gram[course], 0.0)
            at = 256 * course
            gbc_out[:, at : at + 128] = mm(gg.astype(BF16), bc[:, at + 128 : at + 256])
            crossed = jnp.where(sd == course, 0.0, grad_c[...])
            gbc_out[:, at + 128 : at + 256] = mm(gg.T.astype(BF16), bc[:, at : at + 128]) + crossed


def back_cross_kernel(
    sel, adjoint, bc, ksp, z_ref, rate, leaving, sized, xlo, xhi, gxw, sums_in, gbc_in,
    gx_own, gx_sent, grad_out, sums, grads
):
    step = pl.program_id(0)
    lanes = xlo.shape[1]
    tokens = bc.shape[0]
    core, sd = sel[0], sel[1]
    rd = 1 - sd
    heads = lanes // 64

    @pl.when(step == 0)
    def _():
        sums[...] = jnp.zeros_like(sums)
        grads[...] = jnp.zeros_like(grads)

    x = jnp.concatenate([xlo[...], xhi[...]], axis=0).astype(F32)
    b_rows = jnp.where(sd == 0, bc[:, :128], bc[:, 256:384])
    met = mm(b_rows, adjoint[...])
    size = sized[...].astype(F32)
    grad_x = (gxw[...].astype(F32) + size * met).astype(BF16)
    low, high = grad_x[: tokens // 2], grad_x[tokens // 2 :]
    gx_own[...] = jnp.where(core == 0, low, high)
    gx_sent[...] = jnp.where(core == 0, high, low)
    product = x * met * leaving[...].astype(F32)
    shape = (lanes, 128)
    row, col = iota(shape, 0), iota(shape, 1)
    target = sd * 32 + step * heads + ((row & (lanes - 1)) >> 6)
    sums[...] += mm(product.astype(BF16), as_bf16(col == target))
    ve = (x * size).astype(BF16)
    grads[...] += mm_nt(ve, adjoint[...])

    @pl.when(step == pl.num_programs(0) - 1)
    def _():
        within = sums_in[...]
        cross = sums[...]
        size4 = ksp[:, :128].astype(F32) + ksp[:, 128:256].astype(F32) + ksp[:, 256:].astype(F32)
        lane = iota((tokens, 128), 1)
        size4 = jnp.where(lane < 64, pltpu.roll(size4, 64, 1), size4)
        moved = pltpu.roll(within, 64, 1)
        rs = within + cross
        grad_k = moved - size4 * rs
        r_total = jnp.sum(size4 * cross, axis=0, keepdims=True)
        trow, tcol = iota((tokens, tokens), 0), iota((tokens, tokens), 1)
        later = exact_sum(as_bf16(tcol >= trow), grad_k)
        earlier = exact_sum(as_bf16(tcol <= trow), grad_k)
        grad_g = jnp.where(lane < 32, later, earlier) + r_total
        sigma = 1.0 / (1.0 + jnp.exp(-z_ref[...]))
        grad_z = jnp.where(lane < 64, (rs - rate[...] * grad_g) * sigma, 0.0)

        def place(row_at, col_at):
            return (row_at < 64) & (col_at == ((row_at >> 5) & 1) * 64 + core * 32 + (row_at & 31))

        grad_out[:, 512:640] = pick(grad_z, place, 3)
        gbc = gbc_in[...]
        grad_out[:, 0:128] = gbc[:, 0:128] + jnp.where(sd == 0, grads[...], 0.0)
        grad_out[:, 128:256] = gbc[:, 128:256]
        grad_out[:, 256:384] = gbc[:, 256:384] + jnp.where(sd == 1, grads[...], 0.0)
        grad_out[:, 384:512] = gbc[:, 384:512]


def shaped(shape, dtype):
    return jax.ShapeDtypeStruct(shape, dtype)


SMEM = pl.BlockSpec(memory_space=pltpu.SMEM)


def whole(array):
    rank = len(array.shape)
    return pl.BlockSpec(array.shape, lambda *_: (0,) * rank)


def lanes_block(rows, lanes):
    return pl.BlockSpec((rows, lanes), lambda i: (0, i))


def call(body, mega_flops, grid, in_specs, out_specs, out_shape, scratch=()):
    return pl.pallas_call(
        body,
        grid=grid,
        in_specs=in_specs,
        out_specs=out_specs,
        out_shape=out_shape,
        scratch_shapes=list(scratch),
        cost_estimate=pl.CostEstimate(flops=mega_flops * 1000000, bytes_accessed=0, transcendentals=0),
        compiler_params=pltpu.CompilerParams(vmem_limit_bytes=VMEM_LIMIT),
    )


def ring(count, distance):
    return [(i, (i + distance) % count) for i in range(count)]


def swapped(value, axis):
    return lax.ppermute(value, axis, [(0, 1), (1, 0)])


def gather_along_z(weight, count):
    half = count // 2
    slots = []
    for i in range(half):
        route = []
        for z in range(count):
            route.append((2 * z, 2 * ((z + half - 1 - i) % count)))
            route.append((2 * z + 1, 2 * ((z - i - 1) % count) + 1))
        slots.append(lax.ppermute(weight, ("z", "c"), route))
    return slots


def with_x(value, count):
    return jnp.concatenate([value] + [lax.ppermute(value, "x", ring(count, k)) for k in range(1, count)], axis=0)


def over_yh(value):
    return lax.ppermute(value, ("yh", "yl"), [(i, 3 - i) for i in range(4)])


def with_yh(value):
    return jnp.concatenate([value, over_yh(value)], axis=0)


def sum_over_x(value, count):
    total = value[:, 0].astype(F32)
    for k in range(1, count):
        total = total + lax.ppermute(value[:, k], "x", ring(count, k)).astype(F32)
    return total


def shards(sizes, layer_input, head_input, targets, proj_weight, rates, dt_bias, mask_index):
    nz, nx, nyh = sizes
    z, x, yh = (lax.axis_index(name) for name in ("z", "x", "yh"))
    yl, core = lax.axis_index("yl"), lax.axis_index("c")
    tokens, depth = layer_input.shape
    features = head_input.shape[1]
    wide = features // 2
    rows, columns = proj_weight.shape
    chip = 2 * tokens
    quarter = rows // 4
    sel = jnp.stack([core, yl, 2 * (yl ^ yh) + core, z, x, yh]).astype(jnp.int32)

    slots = gather_along_z(proj_weight, nz)

    half_shape = shaped((tokens, depth // 2), BF16)
    quarter_shape = shaped((tokens, depth // 4), BF16)

    def rank_body(*refs):
        rank_kernel(*refs, sizes=sizes)

    outs = [half_shape, half_shape] + [quarter_shape] * 4
    mine, theirs, *quarters = call(
        rank_body, 2640, (), [SMEM, whole(layer_input)], [whole(a) for a in outs], outs
    )(sel, layer_input)

    def own_heads(array):
        own = lax.dynamic_slice_in_dim(array, core * wide, wide, axis=1)
        return own, lax.dynamic_slice_in_dim(array, (1 - core) * wide, wide, axis=1)

    def ordered(own, other):
        return jnp.where(core == 0, own, other), jnp.where(core == 0, other, own)

    def by_core(table):
        own = lax.dynamic_slice_in_dim(table, core * 32, 32, axis=1).reshape(1, 64)
        return jnp.concatenate([own, own], axis=1)

    x_own, x_sent = own_heads(head_input)
    x_other = swapped(x_sent, "c")
    first = jnp.concatenate(slots[: nz // 4], axis=0)
    second = jnp.concatenate(slots[nz // 4 :], axis=0)
    first, second, theirs, x_other = lax.optimization_barrier((first, second, theirs, x_other))
    theirs = swapped(theirs, "c")
    first = with_yh(first)
    second = with_x(second, nx)
    first, second, theirs, quarters[2], quarters[3] = lax.optimization_barrier(
        (first, second, theirs, quarters[2], quarters[3])
    )
    group = {0: quarters[0]}
    for k in (2, 3):
        group[k] = lax.ppermute(quarters[k], SEQ, [(i, i ^ k) for i in range(4)])
    part_a = with_x(first, nx)
    part_b = with_yh(second)
    xlo, xhi = ordered(x_own, x_other)
    chip_input = jnp.concatenate(ordered(mine, theirs), axis=0)
    bias4, rate4 = by_core(dt_bias), by_core(rates)
    part_a, part_b, chip_input, xlo, xhi, bias4, rate4, quarters[1], group[2], group[3] = (
        lax.optimization_barrier(
            (part_a, part_b, chip_input, xlo, xhi, bias4, rate4, quarters[1], group[2], group[3])
        )
    )
    group[1] = swapped(quarters[1], "c")

    span = depth // 4
    projected = jnp.dot(chip_input[:, :span], part_a, preferred_element_type=F32) + jnp.dot(
        chip_input[:, span:], part_b, preferred_element_type=F32
    )
    projected_other = swapped(projected, "c")

    lanes = 64 * GROUP
    steps = wide // lanes
    outs = [
        shaped((chip, 512), BF16),
        shaped((chip, 384), BF16),
        shaped((chip, 128), F32),
        shaped((128, chip), F32),
        shaped((chip, 128), F32),
        shaped((chip, 128), F32),
        shaped((128, wide), BF16),
    ]
    ins = [projected, projected_other, xlo, xhi, bias4, rate4]
    bc, ksp, ks, kt, fac, z4, leaving = call(
        prepare_kernel, 3190, (), [SMEM] + [whole(a) for a in ins], [whole(a) for a in outs], outs
    )(sel, *ins)
    targets, bc = lax.optimization_barrier((targets, bc))
    goal_own, goal_sent = own_heads(targets)
    glo, ghi = ordered(goal_own, swapped(goal_sent, "c"))
    state = swapped(leaving, "yl")

    kt4 = kt[:64].reshape(2, steps, GROUP, chip)
    kt_spec = pl.BlockSpec((2, 1, GROUP, chip), lambda i: (0, i, 0, 0))
    big = lanes_block(chip, lanes)
    small = lanes_block(tokens, lanes)
    state_spec = lanes_block(128, lanes)
    wide_shape = shaped((chip, wide), BF16)
    wide_half = shaped((tokens, wide), BF16)
    square = pltpu.VMEM((2, chip, chip), F32)
    tables = pltpu.VMEM((2, 256, lanes), BF16)
    y_sd, y_rd, entering = call(
        within_kernel, 6160,
        (steps,),
        [SMEM, whole(ks), kt_spec, whole(fac), whole(bc), small, small],
        [big] * 3,
        [wide_shape] * 3,
        [square, tables],
    )(sel, ks, kt4, fac, bc, xlo, xhi)


    stats_shape = shaped((chip, 128), F32)
    y, stats = call(
        cross_kernel, 3080,
        (steps,),
        [SMEM, whole(bc), big, state_spec, big, big, small, small],
        [big, whole(stats_shape)],
        [wide_shape, stats_shape],
        [pltpu.VMEM((3, chip, 128), F32)],
    )(sel, bc, entering, state, y_sd, y_rd, glo, ghi)
    stats_other = swapped(stats, "c")

    def loss_body(*refs):
        loss_kernel(*refs, count=features)

    go, direct = call(
        loss_body, 3300,
        (steps,),
        [SMEM, whole(stats), whole(stats), whole(mask_index), whole(bc), big, big, small, small],
        [big, state_spec],
        [wide_shape, shaped((128, wide), BF16)],
        [pltpu.VMEM((chip, 128), F32), pltpu.VMEM((chip, 128), F32)],
    )(sel, stats, stats_other, mask_index, bc, entering, y, glo, ghi)
    adjoint = swapped(direct, "yl")
    group_input = jnp.concatenate(ordered(group[0], group[1]) + ordered(group[2], group[3]), axis=0)

    gbc_shape = shaped((chip, 512), F32)
    gxw, sums, gbc, leaving, sized = call(
        back_within_kernel, 12650,
        (steps,),
        [SMEM, whole(ks), kt_spec, whole(fac), whole(bc), small, small, big, big, big, big, state_spec],
        [big, whole(stats_shape), whole(gbc_shape), big, big],
        [wide_shape, stats_shape, gbc_shape, wide_shape, wide_shape],
        [square, tables, square]
        + [pltpu.VMEM((chip, 128), F32)] * 2
        + [pltpu.VMEM((4 * lanes, 128), BF16)],
    )(sel, ks, kt4, fac, bc, xlo, xhi, go, y, y_sd, entering, state)

    grad_shape = shaped((chip, columns), F32)
    gx_own, gx_sent, grad = call(
        back_cross_kernel, 4950,
        (steps,),
        [SMEM, state_spec]
        + [whole(a) for a in (bc, ksp, z4, rate4)]
        + [big, big, small, small, big, whole(sums), whole(gbc)],
        [small, small, whole(grad_shape)],
        [wide_half, wide_half, grad_shape],
        [pltpu.VMEM((chip, 128), F32), pltpu.VMEM((chip, 128), F32)],
    )(sel, adjoint, bc, ksp, z4, rate4, leaving, sized, xlo, xhi, gxw, sums, gbc)

    def by_owner(low, high):
        return jnp.where(core == 0, low, high), jnp.where(core == 0, high, low)

    grad_proj = (grad + swapped(grad, "c")).astype(BF16)
    far = swapped(by_owner(grad_proj[:tokens], grad_proj[tokens:])[0], "yl")
    grad_group = jnp.concatenate((grad_proj,) + by_owner(far, swapped(far, "c")), axis=0)

    def weight_rows(columns_at):
        value = lax.dot_general(
            columns_at, grad_group, (((0,), (0,)), ((), ())), preferred_element_type=F32
        ).astype(BF16)
        return value.reshape(-1, nx, nyh, quarter, columns)

    cut = (5 * nz // 8) * (depth // 4 // nz)
    second = weight_rows(group_input[:, cut:])
    second = second[:, :, 0].astype(F32) + over_yh(second[:, :, 1]).astype(F32)
    first = weight_rows(group_input[:, :cut])
    first = sum_over_x(first, nx).astype(BF16)
    second = sum_over_x(second.astype(BF16), nx)
    first = first[:, 0].astype(F32) + over_yh(first[:, 1]).astype(F32)
    total = jnp.concatenate([first, second], axis=0).astype(BF16)
    total = lax.all_to_all(total, "z", 0, 0, tiled=True)
    total = jnp.sum(total.astype(F32), axis=0)
    grad_weight = lax.all_gather(
        total, ("yh",) + SEQ, axis=0, tiled=True, axis_index_groups=[[0, 1, 2, 3], [6, 7, 4, 5]]
    )

    def owned_and_received(value):
        own, sent = by_owner(value[:tokens], value[tokens:])
        return own, swapped(sent, "c")

    grad_x = jnp.concatenate(by_owner(gx_own, swapped(gx_sent, "c")), axis=1)

    wide_grad = jnp.concatenate(
        [
            lax.dot_general(grad_proj, part, (((1,), (1,)), ((), ())), preferred_element_type=F32).astype(BF16)
            for part in (part_a, part_b)
        ],
        axis=1,
    )

    def unrank_body(*refs):
        unrank_kernel(*refs, sizes=sizes)

    grad_input = call(
        unrank_body, 2200,
        (),
        [SMEM, whole(half_shape), whole(half_shape)],
        whole(layer_input),
        shaped(layer_input.shape, BF16),
    )(sel, *owned_and_received(wide_grad))
    return grad_x, grad_input, grad_weight


def solution(mesh):
    sizes = fsdp_axes(mesh.shape["fsdp"])
    fine = Mesh(np.asarray(mesh.devices).reshape(*sizes, 2, 2), ("z", "x", "yh", "yl", "c"))
    fsdp = ("z", "x", "yh")
    tokens = P(fsdp + SEQ, None)
    rows = P(fsdp, None)

    def body(*arrays):
        return shards(sizes, *arrays)

    return jax.shard_map(
        body,
        mesh=fine,
        in_specs=(tokens, tokens, tokens, rows, P(), P(), rows),
        out_specs=(tokens, tokens, rows),
        check_vma=False,
    )
```

```python
import jax
import jax.numpy as jnp
import numpy as np
from jax import lax
from jax.experimental import pallas as pl
from jax.experimental.pallas import tpu as pltpu
from jax.sharding import Mesh
from jax.sharding import PartitionSpec as P

EPSILON = 1e-06
LOG2E = 1.4426950408889634
F32 = jnp.float32
BF16 = jnp.bfloat16
SEQ = ("yl", "c")
VMEM_LIMIT = 14 * 1024 * 1024
GROUP = 8


def fsdp_axes(count):
    return (count // 8, 4, 2)


def iota(shape, dim):
    return lax.broadcasted_iota(jnp.int32, shape, dim)


def mm(left, right):
    return lax.dot_general(left, right, (((1,), (0,)), ((), ())), preferred_element_type=F32)


def mm_nt(left, right):
    return lax.dot_general(left, right, (((1,), (1,)), ((), ())), preferred_element_type=F32)


def parts(value, count):
    pieces = []
    for _ in range(count):
        piece = value.astype(BF16)
        pieces.append(piece)
        value = value - piece.astype(F32)
    return jnp.concatenate(pieces, axis=1)


def as_bf16(condition):
    return jnp.where(condition, 1.0, 0.0).astype(BF16)


def exact_sum(mask, value):
    width = value.shape[1]
    out = mm(mask, parts(value, 3))
    return out[:, :width] + out[:, width : 2 * width] + out[:, 2 * width :]


def pick(value, chosen, pieces):
    rows, width = value.shape
    table = as_bf16(chosen(iota((pieces * width, width), 0) & (width - 1), iota((pieces * width, width), 1)))
    return mm(parts(value, pieces), table)


def spread_table(pieces, lane_base, lanes):
    shape = (pieces * 128, lanes)
    return as_bf16((iota(shape, 0) & 127) == lane_base + (iota(shape, 1) >> 6))


def block_at(z, core, i, count):
    half = count // 2
    return (jnp.where(core == 0, z + count - (half - 1 - i), z + i + 1)) & (count - 1)


def rank_kernel(sel, rows_in, mine, theirs, *quarters, sizes):
    nz, nx, nyh = sizes
    core, member, z, x, yh = sel[0], sel[2], sel[3], sel[4], sel[5]
    tokens = rows_in.shape[0]
    block = 128 * nx
    low_lanes = iota((tokens, 128), 1) < 64
    for out, owner in ((mine, core), (theirs, 1 - core)):
        for part in range(2):
            starts = [block_at(z, owner, 2 * part + i, nz) * block for i in range(2)]
            for xr in range(nx):
                at = ((x + nx - xr) & (nx - 1)) * 128
                tiles = [rows_in[:, pl.ds(pl.multiple_of(start + at, 128), 128)].astype(F32) for start in starts]
                low = jnp.where(low_lanes, tiles[0], pltpu.roll(tiles[1], 64, 1))
                high = jnp.where(low_lanes, pltpu.roll(tiles[0], 64, 1), tiles[1])
                for yr in range(nyh):
                    place = (xr * nyh + yr) if part == 0 else (yr * nx + xr)
                    to = part * 2 * block + place * 128
                    out[:, to : to + 128] = jnp.where(yh == yr, low, high).astype(BF16)
    dst = iota((1, block), 1)
    xr, yr = (dst >> 5) & (nx - 1), (dst >> 4) & 1
    source = ((x + xr) & (nx - 1)) * 128 + (yh ^ yr) * 64 + (member ^ (dst >> 7)) * 16 + (dst & 15)
    table = as_bf16(iota((block, block), 0) == source)
    for zz in range(nz):
        value = mm(rows_in[:, zz * block : (zz + 1) * block], table).astype(BF16)
        for k, out in enumerate(quarters):
            out[:, zz * 128 : (zz + 1) * 128] = value[:, k * 128 : (k + 1) * 128]


def unrank_kernel(sel, mine, theirs, out, *, sizes):
    nz, nx, nyh = sizes
    core, z, x, yh = sel[0], sel[3], sel[4], sel[5]
    tokens = out.shape[0]
    block = 128 * nx
    low_lanes = iota((tokens, 128), 1) < 64
    for ref, owner in ((mine, core), (theirs, 1 - core)):
        for part in range(2):
            starts = [block_at(z, owner, 2 * part + i, nz) * block for i in range(2)]
            for xr in range(nx):
                at = ((x + nx - xr) & (nx - 1)) * 128
                pair = []
                for yr in range(nyh):
                    place = (xr * nyh + yr) if part == 0 else (yr * nx + xr)
                    to = part * 2 * block + place * 128
                    pair.append(ref[:, to : to + 128].astype(F32))
                low = jnp.where(yh == 0, pair[0], pair[1])
                high = jnp.where(yh == 0, pair[1], pair[0])
                first = jnp.where(low_lanes, low, pltpu.roll(high, 64, 1))
                second = jnp.where(low_lanes, pltpu.roll(low, 64, 1), high)
                for start, tile in zip(starts, (first, second)):
                    out[:, pl.ds(pl.multiple_of(start + at, 128), 128)] = tile.astype(BF16)


def prepare_kernel(sel, pa, pb, xlo, xhi, bias, rate, bc_out, ksp_out, ks_out, kt_out, fac_out, z_out, state_out):
    tokens = pa.shape[0]
    core, sd = sel[0], sel[1]
    proj = pa[...] + pb[...]
    bc = proj[:, :512].astype(BF16)
    bc_out[...] = bc

    def source(row, col):
        return row == ((col >> 5) & 1) * 64 + core * 32 + (col & 31)

    z = pick(proj[:, 512:640], source, 3) + bias[...]
    z_out[...] = z
    step = jnp.maximum(z, 0.0) + jnp.log1p(jnp.exp(-jnp.abs(z)))
    g = -rate[...] * step * LOG2E
    row = iota((tokens, tokens), 0)
    col = iota((tokens, tokens), 1)
    low = exact_sum(as_bf16(col <= row), g)
    high = exact_sum(as_bf16(col >= row), g)
    lane = iota((tokens, 128), 1)
    first = ((lane >> 5) & 1) == 0
    k = jnp.where(first, low, high)
    total = jnp.where(first[:1], low[tokens - 1 :], high[:1])
    ks = jnp.where(lane < 64, k, step)
    ksp_out[...] = parts(ks, 3)
    kt_out[...] = ks.T
    ks_out[...] = ks
    leaving = jnp.exp2(total - k)
    fac_out[...] = jnp.where(lane < 64, jnp.exp2(k), leaving)
    factor = parts(step * leaving, 2)
    b_t = jnp.where(sd == 0, proj[:, :128], proj[:, 256:384]).T.astype(BF16)
    width = xlo.shape[1]
    for at in range(0, width, 256):
        table = spread_table(2, sd * 32 + at // 64, 256)
        x = jnp.concatenate([xlo[:, at : at + 256], xhi[:, at : at + 256]], axis=0)
        ve = (x.astype(F32) * mm(factor, table)).astype(BF16)
        state_out[:, at : at + 256] = mm(b_t, ve).astype(BF16)


def halves(value):
    first = (iota(value.shape, 1) & 64) == 0
    zero = jnp.zeros_like(value)
    return jnp.where(first, value, zero), jnp.where(first, zero, value)


def set_up(gram, tables, bc, lanes, transposed):
    half = bc.shape[0] // 2
    shape = (2 * half, 2 * half)
    row, col = iota(shape, 0), iota(shape, 1)
    for course in range(2):
        b_rows = bc[:, 256 * course : 256 * course + 128]
        c_rows = bc[:, 256 * course + 128 : 256 * course + 256]
        value = mm_nt(b_rows, c_rows) if transposed else mm_nt(c_rows, b_rows)
        keep = col <= row if (course == 0) != transposed else col >= row
        gram[course] = jnp.where(keep, value, 0.0)
        tables[course] = spread_table(2, 64 + 32 * course, lanes)


def within_kernel(sel, ks_ref, kt, fac, bc, xlo, xhi, y_sd, y_rd, entering, gram, tables):
    half = bc.shape[0] // 2
    sd = sel[1]

    @pl.when(pl.program_id(0) == 0)
    def _():
        set_up(gram, tables, bc, xlo.shape[1], False)

    x = jnp.concatenate([xlo[...], xhi[...]], axis=0).astype(F32)
    ks = pltpu.roll(ks_ref[...], 128 - GROUP * pl.program_id(0), 1)
    ks_parts = parts(ks, 2)
    results = []
    for course in range(2):
        v_a, v_b = halves((x * mm(ks_parts, tables[course])).astype(BF16))
        by_rows = []
        for tb in range(2):
            t_at = slice(tb * half, (tb + 1) * half)
            sources = range(tb + 1) if course == 0 else range(tb, 2)
            weights = [[] for _ in range(GROUP // 2)]
            values = [[] for _ in range(GROUP // 2)]
            for sb in sources:
                s_at = slice(sb * half, (sb + 1) * half)
                table = gram[course, t_at, s_at]
                for head in range(GROUP):
                    lane = 32 * course + head
                    gap = ks[t_at, lane : lane + 1] - kt[course, 0, head : head + 1, s_at]
                    if tb == sb:
                        gap = jnp.minimum(gap, 0.0)
                    pair = head // 2
                    weights[pair].append((jnp.exp2(gap) * table).astype(BF16))
                    values[pair].append((v_a, v_b)[head % 2][s_at, 128 * pair : 128 * pair + 128])
            by_rows.append(
                jnp.concatenate(
                    [
                        mm(jnp.concatenate(w, axis=1), jnp.concatenate(v, axis=0))
                        for w, v in zip(weights, values)
                    ],
                    axis=1,
                )
            )
        results.append(jnp.concatenate(by_rows, axis=0))
    y_sd[...] = jnp.where(sd == 0, results[0], results[1]).astype(BF16)
    y_rd[...] = jnp.where(sd == 0, results[1], results[0]).astype(BF16)
    factors = parts(fac[...], 2)
    lanes = xlo.shape[1]
    base = GROUP * pl.program_id(0)
    entering[...] = mm(factors, spread_table(2, (1 - sd) * 32 + base, lanes)).astype(BF16)


def cross_kernel(sel, bc, entering, state, y_sd, y_rd, glo, ghi, y_out, stats, acc):
    step = pl.program_id(0)
    lanes = state.shape[1]
    rd = 1 - sel[1]
    c_rows = jnp.where(rd == 0, bc[:, 128:256], bc[:, 384:512])
    carried = entering[...].astype(F32) * mm(c_rows, state[...])
    y = y_sd[...].astype(F32) + y_rd[...].astype(F32) + carried
    y_out[...] = y.astype(BF16)
    t = jnp.concatenate([glo[...], ghi[...]], axis=0).astype(F32)

    @pl.when(step == 0)
    def _():
        acc[...] = jnp.zeros_like(acc)

    for slot, value in enumerate((y * y, y * t, t * t)):
        total = value[:, :128]
        for at in range(128, lanes, 128):
            total = total + value[:, at : at + 128]
        acc[slot] += total

    @pl.when(step == pl.num_programs(0) - 1)
    def _():
        lane = iota(stats.shape, 1)
        out = jnp.zeros(stats.shape, F32)
        for slot in range(3):
            out = jnp.where(lane == slot, jnp.sum(acc[slot], axis=1, keepdims=True), out)
        stats[...] = out


def loss_kernel(sel, own, other, index, bc, entering, y_ref, glo, ghi, go_out, direct_out, y_scale, t_scale, *, count):
    step = pl.program_id(0)
    lanes = glo.shape[1]
    rd = 1 - sel[1]

    @pl.when(step == 0)
    def _():
        stats = (own[...] + other[...]) * (1.0 / count)
        ry = jnp.sqrt(stats[:, 0:1] + EPSILON)
        rt = jnp.sqrt(stats[:, 2:3] + EPSILON)
        cosine = stats[:, 1:2] / (ry * rt)
        position = sel[1] * bc.shape[0] + iota((bc.shape[0], index.shape[1]), 0)
        masked = jnp.max(jnp.where(position == index[...], 1.0, 0.0), axis=1, keepdims=True) > 0.0
        y_scale[...] = jnp.broadcast_to(jnp.where(masked, cosine / (ry * ry), 0.0), y_scale.shape)
        t_scale[...] = jnp.broadcast_to(jnp.where(masked, 1.0 / (rt * ry), 0.0), t_scale.shape)

    wide = (1, lanes // 128)
    t = jnp.concatenate([glo[...], ghi[...]], axis=0).astype(F32)
    y = y_ref[...].astype(F32)
    go = (jnp.tile(y_scale[...], wide) * y - jnp.tile(t_scale[...], wide) * t).astype(BF16)
    go_out[...] = go
    go_f = go.astype(F32)
    scaled = (entering[...].astype(F32) * go_f).astype(BF16)
    c_t = jnp.where(rd == 0, bc[:, 128:256], bc[:, 384:512]).astype(F32).T.astype(BF16)
    direct_out[...] = mm(c_t, scaled).astype(BF16)


def place_table(lanes):
    shape = (4 * lanes, 128)
    row = iota(shape, 0)
    return as_bf16(iota(shape, 1) == (row // lanes) * 32 + ((row & (lanes - 1)) >> 6))


def back_within_kernel(
    sel, ks_ref, kt, fac, bc, xlo, xhi, go_ref, y_ref, y_sd, entering, state,
    gx_out, sums_out, gbc_out, leaving, sized, gram, tables, grad_gram, sums, grad_c, place
):
    half = bc.shape[0] // 2
    step_at = pl.program_id(0)
    lanes = xlo.shape[1]
    sd = sel[1]

    @pl.when(step_at == 0)
    def _():
        set_up(gram, tables, bc, lanes, True)
        place[...] = place_table(lanes)
        grad_c[...] = jnp.zeros_like(grad_c)
        grad_gram[...] = jnp.zeros_like(grad_gram)
        sums[...] = jnp.zeros_like(sums)

    x = jnp.concatenate([xlo[...], xhi[...]], axis=0).astype(F32)
    go = go_ref[...]
    go_heads = halves(go)
    ks = pltpu.roll(ks_ref[...], 128 - GROUP * pl.program_id(0), 1)
    ks_parts = parts(ks, 2)
    grad_x = None
    products = []
    for course in range(2):
        step = mm(ks_parts, tables[course])
        v_heads = halves((x * step).astype(BF16))
        by_rows = []
        for sb in range(2):
            s_at = slice(sb * half, (sb + 1) * half)
            weights = [[] for _ in range(GROUP // 2)]
            values = [[] for _ in range(GROUP // 2)]
            for tb in (range(sb, 2) if course == 0 else range(sb + 1)):
                t_at = slice(tb * half, (tb + 1) * half)
                table = gram[course, s_at, t_at]
                gained = None
                for head in range(GROUP):
                    pair = head // 2
                    pair_at = slice(128 * pair, 128 * pair + 128)
                    lane = 32 * course + head
                    gap = kt[course, 0, head : head + 1, t_at] - ks[s_at, lane : lane + 1]
                    if tb == sb:
                        gap = jnp.minimum(gap, 0.0)
                    decay = jnp.exp2(gap)
                    weights[pair].append((decay * table).astype(BF16))
                    values[pair].append(go_heads[head % 2][t_at, pair_at])
                    term = mm_nt(v_heads[head % 2][s_at, pair_at], go[t_at, pair_at]) * decay
                    gained = term if gained is None else gained + term
                grad_gram[course, s_at, t_at] += gained
            by_rows.append(
                jnp.concatenate(
                    [
                        mm(jnp.concatenate(w, axis=1), jnp.concatenate(v, axis=0))
                        for w, v in zip(weights, values)
                    ],
                    axis=1,
                )
            )
        grad_v = jnp.concatenate(by_rows, axis=0)
        part = step * grad_v
        grad_x = part if grad_x is None else grad_x + part
        products.append((x * grad_v).astype(BF16))
    gx_out[...] = grad_x.astype(BF16)
    go_f = go.astype(F32)
    own = y_sd[...].astype(F32)
    rest = y_ref[...].astype(F32) - own
    products.append((go_f * jnp.where(sd == 0, own, rest)).astype(BF16))
    products.append((go_f * jnp.where(sd == 0, rest, own)).astype(BF16))
    scaled = (entering[...].astype(F32) * go_f).astype(BF16)
    grad_c[...] += mm_nt(scaled, state[...])
    gained = mm(jnp.concatenate(products, axis=1), place[...])
    sums[...] += pltpu.roll(gained, GROUP * step_at, 1)
    factors = parts(fac[...], 2)
    left = mm(factors, spread_table(2, 64 + sd * 32 + GROUP * step_at, lanes))
    leaving[...] = left.astype(BF16)
    sized[...] = (left * mm(ks_parts, jnp.where(sd == 0, tables[0], tables[1]))).astype(BF16)

    @pl.when(step_at == pl.num_programs(0) - 1)
    def _():
        sums_out[...] = sums[...]
        shape = (2 * half, 2 * half)
        row, col = iota(shape, 0), iota(shape, 1)
        for course in range(2):
            keep = row <= col if course == 0 else row >= col
            gg = jnp.where(keep, grad_gram[course], 0.0)
            at = 256 * course
            gbc_out[:, at : at + 128] = mm(gg.astype(BF16), bc[:, at + 128 : at + 256])
            crossed = jnp.where(sd == course, 0.0, grad_c[...])
            gbc_out[:, at + 128 : at + 256] = mm(gg.T.astype(BF16), bc[:, at : at + 128]) + crossed


def back_cross_kernel(
    sel, adjoint, bc, ksp, z_ref, rate, leaving, sized, xlo, xhi, gxw, sums_in, gbc_in,
    gx_own, gx_sent, grad_out, sums, grads
):
    step = pl.program_id(0)
    lanes = xlo.shape[1]
    tokens = bc.shape[0]
    core, sd = sel[0], sel[1]
    rd = 1 - sd
    heads = lanes // 64

    @pl.when(step == 0)
    def _():
        sums[...] = jnp.zeros_like(sums)
        grads[...] = jnp.zeros_like(grads)

    x = jnp.concatenate([xlo[...], xhi[...]], axis=0).astype(F32)
    b_rows = jnp.where(sd == 0, bc[:, :128], bc[:, 256:384])
    met = mm(b_rows, adjoint[...])
    size = sized[...].astype(F32)
    grad_x = (gxw[...].astype(F32) + size * met).astype(BF16)
    low, high = grad_x[: tokens // 2], grad_x[tokens // 2 :]
    gx_own[...] = jnp.where(core == 0, low, high)
    gx_sent[...] = jnp.where(core == 0, high, low)
    product = x * met * leaving[...].astype(F32)
    shape = (lanes, 128)
    row, col = iota(shape, 0), iota(shape, 1)
    target = sd * 32 + step * heads + ((row & (lanes - 1)) >> 6)
    sums[...] += mm(product.astype(BF16), as_bf16(col == target))
    ve = (x * size).astype(BF16)
    grads[...] += mm_nt(ve, adjoint[...])

    @pl.when(step == pl.num_programs(0) - 1)
    def _():
        within = sums_in[...]
        cross = sums[...]
        size4 = ksp[:, :128].astype(F32) + ksp[:, 128:256].astype(F32) + ksp[:, 256:].astype(F32)
        lane = iota((tokens, 128), 1)
        size4 = jnp.where(lane < 64, pltpu.roll(size4, 64, 1), size4)
        moved = pltpu.roll(within, 64, 1)
        rs = within + cross
        grad_k = moved - size4 * rs
        r_total = jnp.sum(size4 * cross, axis=0, keepdims=True)
        trow, tcol = iota((tokens, tokens), 0), iota((tokens, tokens), 1)
        later = exact_sum(as_bf16(tcol >= trow), grad_k)
        earlier = exact_sum(as_bf16(tcol <= trow), grad_k)
        grad_g = jnp.where(lane < 32, later, earlier) + r_total
        sigma = 1.0 / (1.0 + jnp.exp(-z_ref[...]))
        grad_z = jnp.where(lane < 64, (rs - rate[...] * grad_g) * sigma, 0.0)

        def place(row_at, col_at):
            return (row_at < 64) & (col_at == ((row_at >> 5) & 1) * 64 + core * 32 + (row_at & 31))

        grad_out[:, 512:640] = pick(grad_z, place, 3)
        gbc = gbc_in[...]
        grad_out[:, 0:128] = gbc[:, 0:128] + jnp.where(sd == 0, grads[...], 0.0)
        grad_out[:, 128:256] = gbc[:, 128:256]
        grad_out[:, 256:384] = gbc[:, 256:384] + jnp.where(sd == 1, grads[...], 0.0)
        grad_out[:, 384:512] = gbc[:, 384:512]


def shaped(shape, dtype):
    return jax.ShapeDtypeStruct(shape, dtype)


SMEM = pl.BlockSpec(memory_space=pltpu.SMEM)


def whole(array):
    rank = len(array.shape)
    return pl.BlockSpec(array.shape, lambda *_: (0,) * rank)


def lanes_block(rows, lanes):
    return pl.BlockSpec((rows, lanes), lambda i: (0, i))


def call(body, mega_flops, grid, in_specs, out_specs, out_shape, scratch=()):
    return pl.pallas_call(
        body,
        grid=grid,
        in_specs=in_specs,
        out_specs=out_specs,
        out_shape=out_shape,
        scratch_shapes=list(scratch),
        cost_estimate=pl.CostEstimate(flops=mega_flops * 1000000, bytes_accessed=0, transcendentals=0),
        compiler_params=pltpu.CompilerParams(vmem_limit_bytes=VMEM_LIMIT),
    )


def ring(count, distance):
    return [(i, (i + distance) % count) for i in range(count)]


def swapped(value, axis):
    return lax.ppermute(value, axis, [(0, 1), (1, 0)])


def gather_along_z(weight, count):
    half = count // 2
    slots = []
    for i in range(half):
        route = []
        for z in range(count):
            route.append((2 * z, 2 * ((z + half - 1 - i) % count)))
            route.append((2 * z + 1, 2 * ((z - i - 1) % count) + 1))
        slots.append(lax.ppermute(weight, ("z", "c"), route))
    return slots


def with_x(value, count):
    return jnp.concatenate([value] + [lax.ppermute(value, "x", ring(count, k)) for k in range(1, count)], axis=0)


def over_yh(value):
    return lax.ppermute(value, ("yh", "yl"), [(i, 3 - i) for i in range(4)])


def with_yh(value):
    return jnp.concatenate([value, over_yh(value)], axis=0)


def sum_over_x(value, count):
    total = value[:, 0].astype(F32)
    for k in range(1, count):
        total = total + lax.ppermute(value[:, k], "x", ring(count, k)).astype(F32)
    return total


def shards(sizes, layer_input, head_input, targets, proj_weight, rates, dt_bias, mask_index):
    nz, nx, nyh = sizes
    z, x, yh = (lax.axis_index(name) for name in ("z", "x", "yh"))
    yl, core = lax.axis_index("yl"), lax.axis_index("c")
    tokens, depth = layer_input.shape
    features = head_input.shape[1]
    wide = features // 2
    rows, columns = proj_weight.shape
    chip = 2 * tokens
    quarter = rows // 4
    sel = jnp.stack([core, yl, 2 * (yl ^ yh) + core, z, x, yh]).astype(jnp.int32)

    slots = gather_along_z(proj_weight, nz)

    half_shape = shaped((tokens, depth // 2), BF16)
    quarter_shape = shaped((tokens, depth // 4), BF16)

    def rank_body(*refs):
        rank_kernel(*refs, sizes=sizes)

    outs = [half_shape, half_shape] + [quarter_shape] * 4
    mine, theirs, *quarters = call(
        rank_body, 2640, (), [SMEM, whole(layer_input)], [whole(a) for a in outs], outs
    )(sel, layer_input)

    def own_heads(array):
        own = lax.dynamic_slice_in_dim(array, core * wide, wide, axis=1)
        return own, lax.dynamic_slice_in_dim(array, (1 - core) * wide, wide, axis=1)

    def ordered(own, other):
        return jnp.where(core == 0, own, other), jnp.where(core == 0, other, own)

    def by_core(table):
        own = lax.dynamic_slice_in_dim(table, core * 32, 32, axis=1).reshape(1, 64)
        return jnp.concatenate([own, own], axis=1)

    x_own, x_sent = own_heads(head_input)
    x_other = swapped(x_sent, "c")
    first = jnp.concatenate(slots[: nz // 4], axis=0)
    second = jnp.concatenate(slots[nz // 4 :], axis=0)
    first, second, theirs, x_other = lax.optimization_barrier((first, second, theirs, x_other))
    theirs = swapped(theirs, "c")
    first = with_yh(first)
    second = with_x(second, nx)
    first, second, theirs, quarters[2], quarters[3] = lax.optimization_barrier(
        (first, second, theirs, quarters[2], quarters[3])
    )
    group = {0: quarters[0]}
    for k in (2, 3):
        group[k] = lax.ppermute(quarters[k], SEQ, [(i, i ^ k) for i in range(4)])
    part_a = with_x(first, nx)
    part_b = with_yh(second)
    xlo, xhi = ordered(x_own, x_other)
    chip_input = jnp.concatenate(ordered(mine, theirs), axis=0)
    bias4, rate4 = by_core(dt_bias), by_core(rates)
    part_a, part_b, chip_input, xlo, xhi, bias4, rate4, quarters[1], group[2], group[3] = (
        lax.optimization_barrier(
            (part_a, part_b, chip_input, xlo, xhi, bias4, rate4, quarters[1], group[2], group[3])
        )
    )
    group[1] = swapped(quarters[1], "c")

    span = depth // 4
    projected = jnp.dot(chip_input[:, :span], part_a, preferred_element_type=F32) + jnp.dot(
        chip_input[:, span:], part_b, preferred_element_type=F32
    )
    projected_other = swapped(projected, "c")

    lanes = 64 * GROUP
    steps = wide // lanes
    outs = [
        shaped((chip, 512), BF16),
        shaped((chip, 384), BF16),
        shaped((chip, 128), F32),
        shaped((128, chip), F32),
        shaped((chip, 128), F32),
        shaped((chip, 128), F32),
        shaped((128, wide), BF16),
    ]
    ins = [projected, projected_other, xlo, xhi, bias4, rate4]
    bc, ksp, ks, kt, fac, z4, leaving = call(
        prepare_kernel, 3190, (), [SMEM] + [whole(a) for a in ins], [whole(a) for a in outs], outs
    )(sel, *ins)
    targets, bc = lax.optimization_barrier((targets, bc))
    goal_own, goal_sent = own_heads(targets)
    glo, ghi = ordered(goal_own, swapped(goal_sent, "c"))
    state = swapped(leaving, "yl")

    kt4 = kt[:64].reshape(2, steps, GROUP, chip)
    kt_spec = pl.BlockSpec((2, 1, GROUP, chip), lambda i: (0, i, 0, 0))
    big = lanes_block(chip, lanes)
    small = lanes_block(tokens, lanes)
    state_spec = lanes_block(128, lanes)
    wide_shape = shaped((chip, wide), BF16)
    wide_half = shaped((tokens, wide), BF16)
    square = pltpu.VMEM((2, chip, chip), F32)
    tables = pltpu.VMEM((2, 256, lanes), BF16)
    y_sd, y_rd, entering = call(
        within_kernel, 6160,
        (steps,),
        [SMEM, whole(ks), kt_spec, whole(fac), whole(bc), small, small],
        [big] * 3,
        [wide_shape] * 3,
        [square, tables],
    )(sel, ks, kt4, fac, bc, xlo, xhi)


    light = 2 * lanes
    light_big, light_small, light_state = (lanes_block(rows_of, light) for rows_of in (chip, tokens, 128))
    stats_shape = shaped((chip, 128), F32)
    y, stats = call(
        cross_kernel, 3080,
        (wide // light,),
        [SMEM, whole(bc), light_big, light_state, light_big, light_big, light_small, light_small],
        [light_big, whole(stats_shape)],
        [wide_shape, stats_shape],
        [pltpu.VMEM((3, chip, 128), F32)],
    )(sel, bc, entering, state, y_sd, y_rd, glo, ghi)
    stats_other = swapped(stats, "c")

    def loss_body(*refs):
        loss_kernel(*refs, count=features)

    go, direct = call(
        loss_body, 3300,
        (wide // light,),
        [SMEM, whole(stats), whole(stats), whole(mask_index), whole(bc)]
        + [light_big, light_big, light_small, light_small],
        [light_big, light_state],
        [wide_shape, shaped((128, wide), BF16)],
        [pltpu.VMEM((chip, 128), F32), pltpu.VMEM((chip, 128), F32)],
    )(sel, stats, stats_other, mask_index, bc, entering, y, glo, ghi)
    adjoint = swapped(direct, "yl")
    group_input = jnp.concatenate(ordered(group[0], group[1]) + ordered(group[2], group[3]), axis=0)

    gbc_shape = shaped((chip, 512), F32)
    gxw, sums, gbc, leaving, sized = call(
        back_within_kernel, 12650,
        (steps,),
        [SMEM, whole(ks), kt_spec, whole(fac), whole(bc), small, small, big, big, big, big, state_spec],
        [big, whole(stats_shape), whole(gbc_shape), big, big],
        [wide_shape, stats_shape, gbc_shape, wide_shape, wide_shape],
        [square, tables, square]
        + [pltpu.VMEM((chip, 128), F32)] * 2
        + [pltpu.VMEM((4 * lanes, 128), BF16)],
    )(sel, ks, kt4, fac, bc, xlo, xhi, go, y, y_sd, entering, state)

    grad_shape = shaped((chip, columns), F32)
    gx_own, gx_sent, grad = call(
        back_cross_kernel, 4950,
        (wide // light,),
        [SMEM, light_state]
        + [whole(a) for a in (bc, ksp, z4, rate4)]
        + [light_big, light_big, light_small, light_small, light_big, whole(sums), whole(gbc)],
        [light_small, light_small, whole(grad_shape)],
        [wide_half, wide_half, grad_shape],
        [pltpu.VMEM((chip, 128), F32), pltpu.VMEM((chip, 128), F32)],
    )(sel, adjoint, bc, ksp, z4, rate4, leaving, sized, xlo, xhi, gxw, sums, gbc)

    def by_owner(low, high):
        return jnp.where(core == 0, low, high), jnp.where(core == 0, high, low)

    grad_proj = (grad + swapped(grad, "c")).astype(BF16)
    far = swapped(by_owner(grad_proj[:tokens], grad_proj[tokens:])[0], "yl")
    grad_group = jnp.concatenate((grad_proj,) + by_owner(far, swapped(far, "c")), axis=0)

    def weight_rows(columns_at):
        value = lax.dot_general(
            columns_at, grad_group, (((0,), (0,)), ((), ())), preferred_element_type=F32
        ).astype(BF16)
        return value.reshape(-1, nx, nyh, quarter, columns)

    cut = (5 * nz // 8) * (depth // 4 // nz)
    second = weight_rows(group_input[:, cut:])
    second = second[:, :, 0].astype(F32) + over_yh(second[:, :, 1]).astype(F32)
    first = weight_rows(group_input[:, :cut])
    first = sum_over_x(first, nx).astype(BF16)
    second = sum_over_x(second.astype(BF16), nx)
    first = first[:, 0].astype(F32) + over_yh(first[:, 1]).astype(F32)
    total = jnp.concatenate([first, second], axis=0).astype(BF16)
    total = lax.all_to_all(total, "z", 0, 0, tiled=True)
    total = jnp.sum(total.astype(F32), axis=0)
    grad_weight = lax.all_gather(
        total, ("yh",) + SEQ, axis=0, tiled=True, axis_index_groups=[[0, 1, 2, 3], [6, 7, 4, 5]]
    )

    def owned_and_received(value):
        own, sent = by_owner(value[:tokens], value[tokens:])
        return own, swapped(sent, "c")

    grad_x = jnp.concatenate(by_owner(gx_own, swapped(gx_sent, "c")), axis=1)

    wide_grad = jnp.concatenate(
        [
            lax.dot_general(grad_proj, part, (((1,), (1,)), ((), ())), preferred_element_type=F32).astype(BF16)
            for part in (part_a, part_b)
        ],
        axis=1,
    )

    def unrank_body(*refs):
        unrank_kernel(*refs, sizes=sizes)

    grad_input = call(
        unrank_body, 2200,
        (),
        [SMEM, whole(half_shape), whole(half_shape)],
        whole(layer_input),
        shaped(layer_input.shape, BF16),
    )(sel, *owned_and_received(wide_grad))
    return grad_x, grad_input, grad_weight


def solution(mesh):
    sizes = fsdp_axes(mesh.shape["fsdp"])
    fine = Mesh(np.asarray(mesh.devices).reshape(*sizes, 2, 2), ("z", "x", "yh", "yl", "c"))
    fsdp = ("z", "x", "yh")
    tokens = P(fsdp + SEQ, None)
    rows = P(fsdp, None)

    def body(*arrays):
        return shards(sizes, *arrays)

    return jax.shard_map(
        body,
        mesh=fine,
        in_specs=(tokens, tokens, tokens, rows, P(), P(), rows),
        out_specs=(tokens, tokens, rows),
        check_vma=False,
    )
```
